128 devices in a mesh: row: 8 (over x, y_lo), col: 16 (over z, y_hi, core).
Axes of the slice: x: 4, y: 4 (y_hi: 2, y_lo: 2; y = y_hi * 2 + y_lo), z: 4, core: 2. Of those that a mesh axis runs over, the one named last changes fastest.
Arguments:
- density: bfloat16 [8192, 8192], P('row', 'col'), may hold values from -1.75 to 1.75
- pattern: int32 [64, 64], P('row', 'col'), may hold values from 0 to 1, as said below
- square_filter: int32 [64, 64], P('row', 'col'), may hold values from 0 to 1
- step_filter: int32 [64, 64], P('row', 'col'), may hold values from 0 to 1
Outputs:
- square: bfloat16 [8192, 8192], P('row', 'col')
- stepped: bfloat16 [8192, 8192], P('row', 'col')
The draws below stay inside these ranges and needn't reach their ends.
Inputs may be any that keep to these rules, and one draw needn't show every extreme that they name: Atom blocks sit at positions on a cycle of length 256, block i at 4 p(i) plus 0 to 3, where p is a permutation of the 64 blocks; pattern keeps block pairs whose cycle distance is at most 32, square_filter those within 48, step_filter those within 40, all from the same positions.
All inputs are finite; a program needn't handle non-finite values.
Results may differ from the reference program's by a relative error of at most 0.0049.
Values may be sent and summed in bfloat16 or wider, within the bound.
No kernel may reach another device: no remote copies, remote signals or barrier semaphores. Data moves between devices by JAX's collectives and lax.ppermute only.
A program may use at most 128 MiB of HBM per device.

```python
import jax
import jax.numpy as jnp

BLOCK = 128
NB = 64
NORD = 8192


def cycle_distance(key):
    order = jax.random.permutation(jax.random.fold_in(key, 11), NB).astype(jnp.int32)
    offsets = jax.random.randint(jax.random.fold_in(key, 12), (NB,), 0, 4).astype(jnp.int32)
    places = 4 * order + offsets
    apart = jnp.abs(places[:, None] - places[None, :])
    return jnp.minimum(apart, 4 * NB - apart)


def draw_pattern(key, part):
    spacing = cycle_distance(key)
    return (spacing <= NB // 2).astype(jnp.int32)


def draw_square_filter(key, part):
    spacing = cycle_distance(key)
    return (spacing <= 3 * NB // 4).astype(jnp.int32)


def draw_step_filter(key, part):
    spacing = cycle_distance(key)
    return (spacing <= 5 * NB // 8).astype(jnp.int32)


def level_of(own_key, shape, split, least, top_value):
    def one(dim, blocks):
        heights = jax.random.uniform(jax.random.fold_in(jax.random.fold_in(own_key, 6), dim), (blocks,), jnp.float32, least / len(split), top_value / len(split))
        return jnp.repeat(jnp.exp(heights), shape[dim] // blocks).reshape((-1,) + (1,) * (len(shape) - dim - 1))

    factor_of = one(*split[0])
    for cut in split[1:]:
        factor_of = factor_of * one(*cut)
    return factor_of


def noise(rng, dims, deviation, bound, shards=(), kind=jnp.bfloat16):
    entries = deviation * jax.random.normal(rng, dims, jnp.float32)
    if shards:
        entries = entries * level_of(rng, dims, shards, -0.22, 0.18)
    return jnp.clip(entries, -bound, bound).astype(kind)


def setup_inputs(seed: int = 0) -> dict:
    key_of = jax.random.split(jax.random.key(seed), 5)
    density = noise(key_of[0], (NORD, NORD), ((11.0 / (0.25 * NORD) ** 2) ** (1.0 / 6.0)), 1.75, ((0, 8), (1, 16)))
    pattern = draw_pattern(jax.random.fold_in(key_of[4], 71), 0)
    square_filter = draw_square_filter(jax.random.fold_in(key_of[4], 71), 0)
    step_filter = draw_step_filter(jax.random.fold_in(key_of[4], 71), 0)
    return {"density": density, "pattern": pattern, "square_filter": square_filter, "step_filter": step_filter}


def expand(values, mask):
    rows, cols = values.shape
    shaped = values.reshape(rows // BLOCK, BLOCK, cols // BLOCK, BLOCK)
    return (shaped * mask[:, None, :, None].astype(values.dtype)).reshape(rows, cols)


def reference(density, pattern, square_filter, step_filter):
    masked = expand(density, pattern)
    product = jnp.dot(masked, masked, preferred_element_type=jnp.float32)
    square = expand(product, square_filter).astype(jnp.bfloat16)
    second = jnp.dot(masked, square, preferred_element_type=jnp.float32)
    stepped = 1.5 * masked.astype(jnp.float32) - 0.5 * second
    stepped = expand(stepped, step_filter).astype(jnp.bfloat16)
    return square, stepped
```

```python
import functools

import jax
import jax.numpy as jnp
from jax import lax
from jax.experimental import pallas as pl
from jax.experimental.pallas import tpu as pltpu
from jax.sharding import PartitionSpec as P

BLOCK = 128
NB = 64
TR = 8
TC = 16
SL = 16
KP, KS, KT = 17, 25, 21
SLOTS = KP + 1
PACK = 4 * SLOTS
ZERO = PACK - 1
NONE = NB
VMEM_LIMIT = 40 * 1024 * 1024
BF = jnp.bfloat16


def row_index(x, y):
    return (x % 4) * 2 + (y % 2)


def col_index(z, y, core):
    return (z % 4) * 4 + (y % 2) * 2 + (core % 2)


def row_shift(value, dx, dy):
    pairs = [(row_index(x, y), row_index(x + dx, y + dy)) for x in range(4) for y in range(2)]
    return lax.ppermute(value, "row", pairs)


def col_shift(value, dz, dy, dc):
    pairs = [
        (col_index(z, y, c), col_index(z + dz, y + dy, c + dc))
        for z in range(4)
        for y in range(2)
        for c in range(2)
    ]
    return lax.ppermute(value, "col", pairs)


def pack_kernel(place, sliced, packed, lists, flags, flags_s, sem):
    lane = lax.broadcasted_iota(jnp.int32, (8, BLOCK), 1)
    for s in range(TR):
        flags[8 * s : 8 * s + 8, :] = sliced[s, 8, :, 0:BLOCK].astype(jnp.float32)[0:8].astype(jnp.int32)
    copy = pltpu.make_async_copy(flags, flags_s, sem)
    copy.start()
    packed[...] = jnp.zeros_like(packed)
    for n in range(12):
        for t in range(32):
            lists[n, t] = NONE
    copy.wait()

    def kept(i, counts):
        out = []
        for n in range(4):
            lists[n, counts[n]] = i
            packed[n * SLOTS + counts[n]] = sliced[i // 8, i % 8, :, n * BLOCK : (n + 1) * BLOCK]
            out.append(counts[n] + flags_s[i, n])
        for n in range(4, 12):
            lists[n, counts[n]] = i
            out.append(counts[n] + flags_s[i, n])
        return tuple(out)

    counts = lax.fori_loop(0, NB, kept, (jnp.int32(0),) * 12, unroll=4)
    for n in range(12):
        lists[n, counts[n]] = NONE
    lane = lax.broadcasted_iota(jnp.int32, (SL, BLOCK), 1)
    heads = []
    for g in range(4):
        part = jnp.where(lane < 4, flags[SL * g : SL * (g + 1), :].astype(jnp.float32), 0.0)
        heads.append(pltpu.roll(part, place[1] * 4 + (g % 2) * NB, 1))
    packed[KP] = (heads[0] + heads[1]).astype(BF)
    packed[SLOTS + KP] = (heads[2] + heads[3]).astype(BF)
    packed[2 * SLOTS + KP] = jnp.zeros((SL, BLOCK), BF)
    packed[ZERO] = jnp.zeros((SL, BLOCK), BF)


def fetch_rows(place, parts, rows, sems):
    x, y = place[0] // 2, place[0] % 2
    copies = []
    for dx in range(4):
        for h in range(2):
            d = lax.rem(x - dx + 4, 4) * 2 + (y + h) % 2
            copies.append(pltpu.make_async_copy(parts[dx].at[h], rows.at[:, d], sems.at[2 * dx + h]))
    return copies


def fetch_cols(place, parts, cols, sems):
    z, y, core = place[1] // 4, (place[1] // 2) % 2, place[1] % 2
    copies = []
    for dc in range(2):
        for dz in range(4):
            for h in range(2):
                c = lax.rem(z - dz + 4, 4) * 4 + ((y + h) % 2) * 2 + (core + dc) % 2
                n = len(copies)
                copies.append(
                    pltpu.make_async_copy(parts[4 * dc + dz].at[h], cols.at[pl.ds(c * PACK, PACK)], sems.at[n])
                )
    return copies


def gather_left(table, outer, inner, cols, left, n_outer, n_inner):
    ks = [inner(t) for t in range(n_inner)]

    def one(s, carry):
        i = outer(s)
        at = pl.multiple_of(s * SL, SL)
        for t in range(n_inner):
            left[pl.ds(at, SL), t * BLOCK : (t + 1) * BLOCK] = cols[table[i, ks[t]]]
        return carry

    lax.fori_loop(0, n_outer, one, 0)


def square_kernel(place, lists, *refs):
    row_parts, col_parts = refs[:4], refs[4:12]
    square, table = refs[12:14]
    rows, cols, left, index, sems, sem = refs[14:]
    from_cols = fetch_cols(place, col_parts, cols, sems)
    from_rows = fetch_rows(place, row_parts, rows, sems.at[pl.ds(16, 8)])
    for copy in from_cols + from_rows:
        copy.start()
    for copy in from_cols:
        copy.wait()
    lane = lax.broadcasted_iota(jnp.int32, (SL, BLOCK), 1)
    heads = []
    for slot in (KP, SLOTS + KP):
        head = jnp.zeros((SL, BLOCK), jnp.float32)
        for c in range(TC):
            head = head + cols[c * PACK + slot].astype(jnp.float32)
        heads += [head, pltpu.roll(head, NB, 1)]
    kept = jnp.concatenate([jnp.where(lane < NB, head, 0.0) for head in heads], axis=0)
    before = lax.broadcasted_iota(jnp.int32, (NB, NB), 1) < lax.broadcasted_iota(jnp.int32, (NB, NB), 0)
    rank = jnp.dot(before.astype(jnp.float32).astype(BF), kept.astype(BF), preferred_element_type=jnp.float32)
    slot = lax.broadcasted_iota(jnp.int32, (NB, BLOCK), 1) * SLOTS + rank.astype(jnp.int32)
    index[0:NB, :] = jnp.where(kept > 0.5, slot, ZERO)
    index[NB : NB + 8, :] = jnp.full((8, BLOCK), ZERO, jnp.int32)
    copy = pltpu.make_async_copy(index, table, sem)
    copy.start()
    copy.wait()
    for copy in from_rows:
        copy.wait()
    for j in range(4):
        gather_left(table, lambda s: lists[4 + j, s], lambda t: lists[j, t], cols, left, KS, KP)
        right = rows[j * SLOTS : j * SLOTS + KP].reshape(KP * BLOCK, BLOCK)
        product = jnp.dot(left[...], right, preferred_element_type=jnp.float32)
        square[j * KS : (j + 1) * KS] = product.astype(BF).reshape(KS, SL, BLOCK)


def step_kernel(place, lists, table, *refs):
    row_parts, col_parts = refs[:4], refs[4:12]
    stepped = refs[12]
    rows, cols, left, own, sems = refs[13:]
    copies = fetch_cols(place, col_parts, cols, sems)
    copies += fetch_rows(place, row_parts, rows, sems.at[pl.ds(16, 8)])
    for copy in copies:
        copy.start()
    stepped[...] = jnp.zeros_like(stepped)
    for copy in copies:
        copy.wait()
    for j in range(4):
        gather_left(table, lambda s: lists[8 + j, s], lambda t: lists[4 + j, t], cols, left, KT, KS)
        for s in range(KT):
            own[s] = cols[table[lists[8 + j, s], place[1] * 4 + j]]
        right = rows[j * KS : (j + 1) * KS].reshape(KS * BLOCK, BLOCK)
        product = jnp.dot(left[...], right, preferred_element_type=jnp.float32)
        result = 1.5 * own[...].astype(jnp.float32) - 0.5 * product.reshape(KT, SL, BLOCK)
        own[...] = result.astype(BF)
        for s in range(KT):
            i = lists[8 + j, s]

            @pl.when(i < NB)
            def _():
                stepped[i, :, j * BLOCK : (j + 1) * BLOCK] = own[s]


def square_rows_kernel(place, lists, *refs):
    row_parts = refs[:4]
    out = refs[4]
    rows, sems = refs[5:]
    copies = fetch_rows(place, row_parts, rows, sems)
    for copy in copies:
        copy.start()
    out[...] = jnp.zeros_like(out)
    for copy in copies:
        copy.wait()
    for j in range(4):

        def one(s, carry):
            i = lists[4 + j, s]

            @pl.when(i // 8 == place[0])
            def _():
                out[i % 8, :, :, j * BLOCK : (j + 1) * BLOCK] = rows[j * KS + s]

            return carry

        lax.fori_loop(0, KS, one, 0)


SMEM = pl.BlockSpec(memory_space=pltpu.SMEM)
VMEM = pl.BlockSpec(memory_space=pltpu.VMEM)
ANY = pl.BlockSpec(memory_space=pl.ANY)


def call(kernel, outs, in_specs, out_specs, scratch, flops, moved):
    return pl.pallas_call(
        kernel,
        out_shape=outs,
        in_specs=in_specs,
        out_specs=out_specs,
        scratch_shapes=scratch,
        compiler_params=pltpu.CompilerParams(vmem_limit_bytes=VMEM_LIMIT),
        cost_estimate=pl.CostEstimate(flops=flops, bytes_accessed=moved, transcendentals=0),
    )


def gather_rows(packed):
    both = jnp.stack([packed, row_shift(packed, 0, 1)])
    return [both] + [row_shift(both, dx, 0) for dx in (1, 2, 3)]


def gather_cols(packed):
    both = jnp.stack([packed, col_shift(packed, 0, 1, 0)])
    mine = [both] + [col_shift(both, dz, 0, 0) for dz in (1, 2, 3)]
    return mine + [col_shift(part, 0, 0, 1) for part in mine]


def on_device(density, pattern, square_filter, step_filter):
    place = jnp.stack([lax.axis_index("row"), lax.axis_index("col")]).astype(jnp.int32)
    masks = jnp.concatenate([pattern, square_filter, step_filter], axis=1).astype(BF)
    head = jnp.pad(masks, ((0, SL - 8), (0, 4 * BLOCK - 12)))
    blocks = density.reshape(8, TR, SL, 4 * BLOCK).transpose(1, 0, 2, 3)
    sent = jnp.concatenate([blocks, jnp.broadcast_to(head, (TR, 1, SL, 4 * BLOCK))], axis=1)
    sliced = lax.all_to_all(sent, "row", 0, 0, tiled=True)

    packed, lists = call(
        pack_kernel,
        (jax.ShapeDtypeStruct((PACK, SL, BLOCK), BF), jax.ShapeDtypeStruct((12, 32), jnp.int32)),
        [SMEM, VMEM],
        (VMEM, SMEM),
        [pltpu.VMEM((NB, BLOCK), jnp.int32), pltpu.SMEM((NB, BLOCK), jnp.int32), pltpu.SemaphoreType.DMA],
        0,
        2 << 20,
    )(place, sliced)

    row_parts = gather_rows(packed)
    col_parts = gather_cols(packed)
    square_packed, table = call(
        square_kernel,
        (
            jax.ShapeDtypeStruct((4 * KS, SL, BLOCK), BF),
            jax.ShapeDtypeStruct((NB + 8, BLOCK), jnp.int32),
        ),
        [SMEM, SMEM] + [ANY] * 12,
        (VMEM, SMEM),
        [
            pltpu.VMEM((PACK, TR, SL, BLOCK), BF),
            pltpu.VMEM((TC * PACK, SL, BLOCK), BF),
            pltpu.VMEM((KS * SL, KP * BLOCK), BF),
            pltpu.VMEM((NB + 8, BLOCK), jnp.int32),
            pltpu.SemaphoreType.DMA((24,)),
            pltpu.SemaphoreType.DMA,
        ],
        2 * 4 * KS * SL * KP * BLOCK * BLOCK,
        8 << 20,
    )(place, lists, *row_parts, *col_parts)

    square_parts = gather_rows(square_packed)
    stepped = call(
        step_kernel,
        jax.ShapeDtypeStruct((NB, SL, 4 * BLOCK), BF),
        [SMEM, SMEM, SMEM] + [ANY] * 12,
        VMEM,
        [
            pltpu.VMEM((4 * KS, TR, SL, BLOCK), BF),
            pltpu.VMEM((TC * PACK, SL, BLOCK), BF),
            pltpu.VMEM((KT * SL, KS * BLOCK), BF),
            pltpu.VMEM((KT, SL, BLOCK), BF),
            pltpu.SemaphoreType.DMA((24,)),
        ],
        2 * 4 * KT * SL * KS * BLOCK * BLOCK,
        9 << 20,
    )(place, lists, table, *square_parts, *col_parts)
    back = lax.all_to_all(stepped, "row", 0, 0, tiled=True)
    square = call(
        square_rows_kernel,
        jax.ShapeDtypeStruct((8, TR, SL, 4 * BLOCK), BF),
        [SMEM, SMEM] + [ANY] * 4,
        VMEM,
        [pltpu.VMEM((4 * KS, TR, SL, BLOCK), BF), pltpu.SemaphoreType.DMA((8,))],
        0,
        4 << 20,
    )(place, lists, *square_parts)
    square = square.reshape(8 * BLOCK, 4 * BLOCK)
    stepped = back.reshape(TR, 8, SL, 4 * BLOCK).transpose(1, 0, 2, 3).reshape(8 * BLOCK, 4 * BLOCK)
    return square, stepped


def solution(mesh):
    placed = (P("row", "col"),) * 4
    return jax.shard_map(
        on_device,
        mesh=mesh,
        in_specs=placed,
        out_specs=(P("row", "col"), P("row", "col")),
        check_vma=False,
    )
```

```python
import functools

import jax
import jax.numpy as jnp
from jax import lax
from jax.experimental import pallas as pl
from jax.experimental.pallas import tpu as pltpu
from jax.sharding import PartitionSpec as P

BLOCK = 128
NB = 64
TR = 8
TC = 16
SL = 16
KP, KS, KT = 17, 25, 21
SLOTS = KP + 1
PACK = 4 * SLOTS
ZERO = PACK - 1
NONE = NB
VMEM_LIMIT = 60 * 1024 * 1024
BF = jnp.bfloat16


def row_index(x, y):
    return (x % 4) * 2 + (y % 2)


def col_index(z, y, core):
    return (z % 4) * 4 + (y % 2) * 2 + (core % 2)


def row_shift(value, dx, dy):
    pairs = [(row_index(x, y), row_index(x + dx, y + dy)) for x in range(4) for y in range(2)]
    return lax.ppermute(value, "row", pairs)


def col_shift(value, dz, dy, dc):
    pairs = [
        (col_index(z, y, c), col_index(z + dz, y + dy, c + dc))
        for z in range(4)
        for y in range(2)
        for c in range(2)
    ]
    return lax.ppermute(value, "col", pairs)


def slice_kernel(density, pattern, square_filter, step_filter, sent, small, masks, sems):
    copies = [pltpu.make_async_copy(density.at[:, d], sent.at[d, pl.ds(0, 8)], sems.at[d]) for d in range(TR)]
    filters = [
        pltpu.make_async_copy(mask, masks.at[n], sems.at[TR + n])
        for n, mask in enumerate((pattern, square_filter, step_filter))
    ]
    for copy in filters + copies:
        copy.start()
    small[...] = jnp.zeros_like(small)
    for n, copy in enumerate(filters):
        copy.wait()
        small[4 * n : 4 * n + 4, 0:8] = masks[n].astype(jnp.float32)
    head = small[...].astype(BF)
    for d in range(TR):
        sent[d, 8, :, 0:BLOCK] = head
        sent[d, 8, :, BLOCK:] = jnp.zeros((SL, 3 * BLOCK), BF)
    for copy in copies:
        copy.wait()


def pack_kernel(sliced, packed, lists, flags, flags_s, sem):
    marks = jnp.zeros((SL, BLOCK), jnp.float32)
    for s in range(TR):
        mark = sliced[s, 8, :, 0:BLOCK].astype(jnp.float32)
        marks = marks + (pltpu.roll(mark, 8 * s, 1) if s else mark)
    flags[...] = marks.astype(jnp.int32)
    copy = pltpu.make_async_copy(flags, flags_s, sem)
    copy.start()
    packed[...] = jnp.zeros_like(packed)
    for n in range(4):
        for t in range(KP):
            lists[n, t] = NONE
    copy.wait()

    def kept(b, counts):
        for q in range(8):
            i = 8 * b + q
            out = []
            for n in range(4):
                lists[n, counts[n]] = i
                packed[n * SLOTS + counts[n]] = sliced[b, q, :, n * BLOCK : (n + 1) * BLOCK]
                out.append(counts[n] + flags_s[n, i])
            counts = tuple(out)
        return counts

    counts = lax.fori_loop(0, TR, kept, (jnp.int32(0),) * 4)
    for n in range(4):
        lists[n, counts[n]] = NONE
    packed[KP] = marks.astype(BF)
    packed[ZERO] = jnp.zeros((SL, BLOCK), BF)


def lists_kernel(flags, lists):
    for n in range(8):
        for t in range(KS):
            lists[n, t] = NONE

    def kept(b, counts):
        for q in range(8):
            i = 8 * b + q
            out = []
            for n in range(8):
                lists[n, counts[n]] = i
                out.append(counts[n] + flags[4 + n, i])
            counts = tuple(out)
        return counts

    counts = lax.fori_loop(0, TR, kept, (jnp.int32(0),) * 8)
    for n in range(8):
        lists[n, counts[n]] = NONE


def fetch(parts, layout, target, sems):
    copies = []
    for part, pieces in zip(parts, layout):
        for start, back, line, at, size in pieces:
            n = len(copies)
            copies.append(pltpu.make_async_copy(part.at[pl.ds(start, size)], target(back, line, at, size), sems.at[n]))
    return copies


def fetch_rows(place, parts, layout, rows, sems):
    x, y = place[0] // 2, place[0] % 2

    def target(back, line, at, size):
        return rows.at[pl.ds(at, size), lax.rem(x - back + 4, 4) * 2 + (y + line) % 2]

    return fetch(parts, layout, target, sems)


def fetch_cols(place, parts, layout, cols, sems):
    z, y, core = place[1] // 4, (place[1] // 2) % 2, place[1] % 2

    def target(back, line, at, size):
        line, other = line % 2, line // 2
        c = lax.rem(z - back + 4, 4) * 4 + ((y + line) % 2) * 2 + (core + other) % 2
        return cols.at[pl.ds(c * PACK + at, size)]

    return fetch(parts, layout, target, sems)


def product(table, outer, inner, cols, right):
    total = None
    for t in range(0, len(inner), 2):
        pair = inner[t : t + 2]
        left = jnp.concatenate(
            [jnp.concatenate([cols[table[k, i]] for k in pair], axis=1) for i in outer], axis=0
        )
        part = jnp.dot(left, right(t, len(pair)), preferred_element_type=jnp.float32)
        total = part if total is None else total + part
    return total


def square_kernel(place, inner, outer, *refs):
    row_parts, col_parts = refs[:NR], refs[NR : NR + NC]
    square, table, rows, cols, marks, index, col_sems, row_sems, sem = refs[NR + NC :]
    from_cols = fetch_cols(place, col_parts, COLS, cols, col_sems)
    from_rows = fetch_rows(place, row_parts, ROWS, rows, row_sems)
    for copy in from_cols + from_rows:
        copy.start()
    for copy in from_cols:
        copy.wait()
    for c in range(TC):
        marks[4 * c : 4 * c + 4, :] = cols[c * PACK + KP].astype(jnp.float32)[0:4]
    kept = marks[...]
    before = lax.broadcasted_iota(jnp.int32, (BLOCK, BLOCK), 0) < lax.broadcasted_iota(jnp.int32, (BLOCK, BLOCK), 1)
    rank = jnp.dot(kept.astype(BF), before.astype(jnp.float32).astype(BF), preferred_element_type=jnp.float32)
    slot = lax.broadcasted_iota(jnp.int32, (NB, BLOCK), 0) * SLOTS + rank.astype(jnp.int32)
    index[0:NB, :] = jnp.where(kept > 0.5, slot, ZERO)
    index[NB : NB + 8, :] = jnp.full((8, BLOCK), ZERO, jnp.int32)
    copy = pltpu.make_async_copy(index, table, sem)
    copy.start()
    copy.wait()
    for copy in from_rows:
        copy.wait()

    def column(j, carry):
        def right(t, n):
            return rows[pl.ds(j * SLOTS + t, n)].reshape(n * BLOCK, BLOCK)

        result = product(table, [outer[j, s] for s in range(KS)], [inner[j, t] for t in range(KP)], cols, right)
        square[pl.ds(j * KS, KS)] = result.astype(BF).reshape(KS, SL, BLOCK)
        return carry

    lax.fori_loop(0, 4, column, 0)


def step_kernel(place, inner, table, *refs):
    row_parts, col_parts = refs[:NS], refs[NS : NS + NC]
    stepped, rows, cols, col_sems, row_sems = refs[NS + NC :]
    copies = fetch_cols(place, col_parts, COLS, cols, col_sems)
    copies += fetch_rows(place, row_parts, SQUARES, rows, row_sems)
    for copy in copies:
        copy.start()
    stepped[...] = jnp.zeros_like(stepped)
    for copy in copies:
        copy.wait()
    for j in range(4):

        def right(t, n):
            return rows[j * KS + t : j * KS + t + n].reshape(n * BLOCK, BLOCK)

        outer = [inner[4 + j, s] for s in range(KT)]
        second = product(table, outer, [inner[j, t] for t in range(KS)], cols, right)
        for s, i in enumerate(outer):
            own = cols[table[place[1] * 4 + j, i]].astype(jnp.float32)
            result = 1.5 * own - 0.5 * second[s * SL : (s + 1) * SL]

            @pl.when(i < NB)
            def _():
                stepped[i, :, j * BLOCK : (j + 1) * BLOCK] = result.astype(BF)


def square_rows_kernel(place, lists, *refs):
    row_parts = refs[:NS]
    out, rows, sems = refs[NS:]
    copies = fetch_rows(place, row_parts, SQUARES, rows, sems)
    for copy in copies:
        copy.start()
    out[...] = jnp.zeros_like(out)
    for copy in copies:
        copy.wait()
    for j in range(4):

        def one(s, carry):
            i = lists[j, s]

            @pl.when(i // 8 == place[0])
            def _():
                out[i % 8, :, :, j * BLOCK : (j + 1) * BLOCK] = rows[j * KS + s]

            return carry

        lax.fori_loop(0, KS, one, 0)


SMEM = pl.BlockSpec(memory_space=pltpu.SMEM)
VMEM = pl.BlockSpec(memory_space=pltpu.VMEM)
ANY = pl.BlockSpec(memory_space=pl.ANY)


def call(kernel, outs, in_specs, out_specs, scratch, flops, moved):
    return pl.pallas_call(
        kernel,
        out_shape=outs,
        in_specs=in_specs,
        out_specs=out_specs,
        scratch_shapes=scratch,
        compiler_params=pltpu.CompilerParams(vmem_limit_bytes=VMEM_LIMIT),
        cost_estimate=pl.CostEstimate(flops=flops, bytes_accessed=moved, transcendentals=0),
    )


def apart(slots):
    half = slots // 2
    whole = [(0, 0), (0, 1), (1, 0), (3, 0), (1, 1), (3, 1)]
    layout = [[(0, back, line, 0, slots)] for back, line in whole]
    return layout + [[(0, 2, line, at, half)] for line in range(2) for at in (0, half)]


def merged(slots):
    half = slots // 2
    layout = [[(0, back, line, 0, slots)] for back, line in [(0, 0), (0, 1), (1, 0), (3, 0)]]
    layout += [[(0, 1, 1, 0, slots), (slots, 2, 0, 0, half)], [(0, 3, 1, 0, slots), (slots, 2, 0, half, half)]]
    return layout + [[(0, 2, 1, 0, half)], [(0, 2, 1, half, half)]]


def merged_cores(slots):
    mine = merged(slots)
    swapped = [mine[0], join(mine[1:4]), mine[4], mine[5], join(mine[6:8])]
    return mine + [[(start, back, line + 2, at, size) for start, back, line, at, size in part] for part in swapped]


def join(parts):
    out, begin = [], 0
    for part in parts:
        out += [(begin + start, back, line, at, size) for start, back, line, at, size in part]
        begin += sum(piece[4] for piece in part)
    return out


def ring_apart(packed, shift):
    half = packed.shape[0] // 2
    other = shift(packed, 0, 1)
    left, right = shift(packed, 1, 0), shift(packed, -1, 0)
    other_left, other_right = shift(other, 1, 0), shift(other, -1, 0)
    far = [shift(left[:half], 1, 0), shift(right[half:], -1, 0)]
    far += [shift(other_left[:half], 1, 0), shift(other_right[half:], -1, 0)]
    return [packed, other, left, right, other_left, other_right] + far


def ring_merged(packed, shift):
    slots = packed.shape[0]
    half = slots // 2
    other = shift(packed, 0, 1)
    left, right = shift(packed, 1, 0), shift(packed, -1, 0)
    from_left = shift(jnp.concatenate([other, left[:half]]), 1, 0)
    from_right = shift(jnp.concatenate([other, right[half:]]), -1, 0)
    far = [shift(from_left[:half], 1, 0), shift(from_right[half:slots], -1, 0)]
    return [packed, other, left, right, from_left, from_right] + far


def gather_rows(packed):
    return ring_apart(packed, row_shift)


def gather_cols(packed):
    mine = ring_merged(packed, lambda value, dz, dy: col_shift(value, dz, dy, 0))
    own = [mine[0], jnp.concatenate(mine[1:4]), mine[4], mine[5], jnp.concatenate(mine[6:8])]
    return mine + [col_shift(part, 0, 0, 1) for part in own]


ROWS = merged(PACK)
COLS = merged_cores(PACK)
SQUARES = apart(4 * KS)
NR, NC, NS = len(ROWS), len(COLS), len(SQUARES)


def pieces(layout):
    return sum(len(part) for part in layout)


def on_device(density, pattern, square_filter, step_filter):
    place = jnp.stack([lax.axis_index("row"), lax.axis_index("col")]).astype(jnp.int32)
    sent = call(
        slice_kernel,
        jax.ShapeDtypeStruct((TR, 9, SL, 4 * BLOCK), BF),
        [ANY] * 4,
        VMEM,
        [pltpu.VMEM((SL, BLOCK), jnp.float32), pltpu.VMEM((3, 4, 8), jnp.int32), pltpu.SemaphoreType.DMA((TR + 3,))],
        0,
        2 << 20,
    )(density.reshape(8, TR, SL, 4 * BLOCK), pattern.T, square_filter.T, step_filter.T)
    sliced = lax.all_to_all(sent, "row", 0, 0, tiled=True)

    packed, pattern_lists, flags = call(
        pack_kernel,
        (
            jax.ShapeDtypeStruct((PACK, SL, BLOCK), BF),
            jax.ShapeDtypeStruct((4, 32), jnp.int32),
            jax.ShapeDtypeStruct((SL, BLOCK), jnp.int32),
        ),
        [VMEM],
        (VMEM, SMEM, VMEM),
        [pltpu.SMEM((SL, BLOCK), jnp.int32), pltpu.SemaphoreType.DMA],
        0,
        2 << 20,
    )(sliced)
    lists = call(lists_kernel, jax.ShapeDtypeStruct((8, 32), jnp.int32), [SMEM], SMEM, [], 0, 1 << 14)(flags)

    row_parts = ring_merged(packed, row_shift)
    col_parts = gather_cols(packed)
    square_packed, table = call(
        square_kernel,
        (
            jax.ShapeDtypeStruct((4 * KS, SL, BLOCK), BF),
            jax.ShapeDtypeStruct((NB + 8, BLOCK), jnp.int32),
        ),
        [SMEM] * 3 + [ANY] * (NR + NC),
        (VMEM, SMEM),
        [
            pltpu.VMEM((PACK, TR, SL, BLOCK), BF),
            pltpu.VMEM((TC * PACK, SL, BLOCK), BF),
            pltpu.VMEM((NB, BLOCK), jnp.float32),
            pltpu.VMEM((NB + 8, BLOCK), jnp.int32),
            pltpu.SemaphoreType.DMA((pieces(COLS),)),
            pltpu.SemaphoreType.DMA((pieces(ROWS),)),
            pltpu.SemaphoreType.DMA,
        ],
        2 * 4 * KS * SL * KP * BLOCK * BLOCK,
        8 << 20,
    )(place, pattern_lists, lists, *row_parts, *col_parts)

    square_parts = gather_rows(square_packed)
    stepped = call(
        step_kernel,
        jax.ShapeDtypeStruct((NB, SL, 4 * BLOCK), BF),
        [SMEM] * 3 + [ANY] * (NS + NC),
        VMEM,
        [
            pltpu.VMEM((4 * KS, TR, SL, BLOCK), BF),
            pltpu.VMEM((TC * PACK, SL, BLOCK), BF),
            pltpu.SemaphoreType.DMA((pieces(COLS),)),
            pltpu.SemaphoreType.DMA((pieces(SQUARES),)),
        ],
        2 * 4 * KT * SL * KS * BLOCK * BLOCK,
        9 << 20,
    )(place, lists, table, *square_parts, *col_parts)
    back = lax.all_to_all(stepped, "row", 0, 0, tiled=True)
    square = call(
        square_rows_kernel,
        jax.ShapeDtypeStruct((8, TR, SL, 4 * BLOCK), BF),
        [SMEM, SMEM] + [ANY] * NS,
        VMEM,
        [pltpu.VMEM((4 * KS, TR, SL, BLOCK), BF), pltpu.SemaphoreType.DMA((pieces(SQUARES),))],
        0,
        4 << 20,
    )(place, lists, *square_parts)
    square = square.reshape(8 * BLOCK, 4 * BLOCK)
    stepped = back.reshape(TR, 8, SL, 4 * BLOCK).transpose(1, 0, 2, 3).reshape(8 * BLOCK, 4 * BLOCK)
    return square, stepped


def solution(mesh):
    placed = (P("row", "col"),) * 4
    return jax.shard_map(
        on_device,
        mesh=mesh,
        in_specs=placed,
        out_specs=(P("row", "col"), P("row", "col")),
        check_vma=False,
    )
```

```python
import functools

import jax
import jax.numpy as jnp
from jax import lax
from jax.experimental import pallas as pl
from jax.experimental.pallas import tpu as pltpu
from jax.sharding import PartitionSpec as P

BLOCK = 128
NB = 64
TR = 8
TC = 16
SL = 16
KP, KS, KT = 17, 25, 21
SLOTS = KP + 1
PACK = 4 * SLOTS
ZERO = PACK - 1
NONE = NB
VMEM_LIMIT = 60 * 1024 * 1024
BF = jnp.bfloat16


def row_index(x, y):
    return (x % 4) * 2 + (y % 2)


def col_index(z, y, core):
    return (z % 4) * 4 + (y % 2) * 2 + (core % 2)


def row_shift(value, dx, dy):
    pairs = [(row_index(x, y), row_index(x + dx, y + dy)) for x in range(4) for y in range(2)]
    return lax.ppermute(value, "row", pairs)


def col_shift(value, dz, dy, dc):
    pairs = [
        (col_index(z, y, c), col_index(z + dz, y + dy, c + dc))
        for z in range(4)
        for y in range(2)
        for c in range(2)
    ]
    return lax.ppermute(value, "col", pairs)


def slice_kernel(density, pattern, square_filter, step_filter, sent, small, masks, sems):
    copies = [
        pltpu.make_async_copy(density.at[:, d, :, pl.ds(n * BLOCK, BLOCK)], sent.at[d, pl.ds(8 * n, 8)], sems.at[4 * d + n])
        for d in range(TR)
        for n in range(4)
    ]
    filters = [
        pltpu.make_async_copy(mask, masks.at[n], sems.at[4 * TR + n])
        for n, mask in enumerate((pattern, square_filter, step_filter))
    ]
    for copy in filters + copies:
        copy.start()
    small[...] = jnp.zeros_like(small)
    for n, copy in enumerate(filters):
        copy.wait()
        small[4 * n : 4 * n + 4, 0:8] = masks[n].astype(jnp.float32)
    head = small[...].astype(BF)
    for d in range(TR):
        sent[d, 32] = head
    for copy in copies:
        copy.wait()


def pack_kernel(sliced, packed, lists, flags, flags_s, sem):
    marks = jnp.zeros((SL, BLOCK), jnp.float32)
    for s in range(TR):
        mark = sliced[s, 32].astype(jnp.float32)
        marks = marks + (pltpu.roll(mark, 8 * s, 1) if s else mark)
    flags[...] = marks.astype(jnp.int32)
    copy = pltpu.make_async_copy(flags, flags_s, sem)
    copy.start()
    packed[...] = jnp.zeros_like(packed)
    for n in range(4):
        for t in range(KP):
            lists[n, t] = NONE
    copy.wait()

    def kept(b, counts):
        for q in range(8):
            i = 8 * b + q
            out = []
            for n in range(4):
                lists[n, counts[n]] = i
                packed[n * SLOTS + counts[n]] = sliced[b, 8 * n + q]
                out.append(counts[n] + flags_s[n, i])
            counts = tuple(out)
        return counts

    counts = lax.fori_loop(0, TR, kept, (jnp.int32(0),) * 4)
    for n in range(4):
        lists[n, counts[n]] = NONE
    packed[KP] = marks.astype(BF)
    packed[ZERO] = jnp.zeros((SL, BLOCK), BF)


def lists_kernel(flags, *refs):
    lists = refs[-1]
    for n in range(8):
        for t in range(KS):
            lists[n, t] = NONE

    def kept(b, counts):
        for q in range(8):
            i = 8 * b + q
            out = []
            for n in range(8):
                lists[n, counts[n]] = i
                out.append(counts[n] + flags[4 + n, i])
            counts = tuple(out)
        return counts

    counts = lax.fori_loop(0, TR, kept, (jnp.int32(0),) * 8)
    for n in range(8):
        lists[n, counts[n]] = NONE


def split(layout, slots):
    columns = [[] for _ in range(4)]
    for n, part in enumerate(layout):
        for start, back, line, at, size in part:
            for q in range(0, size, slots):
                columns[(at + q) // slots].append((n, start + q, back, line, at + q, slots))
    return columns


def whole(layout):
    return [(n, *piece) for n, part in enumerate(layout) for piece in part]


def fetch(parts, chosen, target, sems):
    copies = []
    for q, (n, start, back, line, at, size) in enumerate(chosen):
        copies.append(pltpu.make_async_copy(parts[n].at[pl.ds(start, size)], target(back, line, at, size), sems.at[q]))
    return copies


def fetch_rows(place, parts, chosen, rows, sems):
    x, y = place[0] // 2, place[0] % 2

    def target(back, line, at, size):
        return rows.at[pl.ds(at, size), lax.rem(x - back + 4, 4) * 2 + (y + line) % 2]

    return fetch(parts, chosen, target, sems)


def fetch_cols(place, parts, chosen, cols, sems):
    z, y, core = place[1] // 4, (place[1] // 2) % 2, place[1] % 2

    def target(back, line, at, size):
        line, other = line % 2, line // 2
        c = lax.rem(z - back + 4, 4) * 4 + ((y + line) % 2) * 2 + (core + other) % 2
        return cols.at[pl.ds(c * PACK + at, size)]

    return fetch(parts, chosen, target, sems)


def product(table, outer, inner, cols, right):
    total = None
    for t in range(0, len(inner), 2):
        pair = inner[t : t + 2]
        left = jnp.concatenate(
            [jnp.concatenate([cols[table[k, i]] for k in pair], axis=1) for i in outer], axis=0
        )
        part = jnp.dot(left, right(t, len(pair)), preferred_element_type=jnp.float32)
        total = part if total is None else total + part
    return total


def fetch_heads(place, parts, heads, sems):
    z, y, core = place[1] // 4, (place[1] // 2) % 2, place[1] % 2
    copies = []
    for n, start, back, line, at, size in whole(COLS):
        if at <= KP < at + size:
            c = lax.rem(z - back + 4, 4) * 4 + ((y + line % 2) % 2) * 2 + (core + line // 2) % 2
            copies.append(pltpu.make_async_copy(parts[n].at[start + KP - at], heads.at[c], sems.at[len(copies)]))
    return copies


def square_kernel(place, inner, outer, *refs):
    row_parts, col_parts = refs[:NR], refs[NR : NR + NC]
    square, table, rows, cols, marks, heads, index, col_sems, row_sems, head_sems, sem = refs[NR + NC :]
    from_heads = fetch_heads(place, col_parts, heads, head_sems)
    from_cols = fetch_cols(place, col_parts, whole(COLS), cols, col_sems)
    from_rows = fetch_rows(place, row_parts, whole(ROWS), rows, row_sems)
    for copy in from_heads + from_cols + from_rows:
        copy.start()
    for copy in from_heads:
        copy.wait()
    for c in range(TC):
        marks[4 * c : 4 * c + 4, :] = heads[c].astype(jnp.float32)[0:4]
    kept = marks[...]
    before = lax.broadcasted_iota(jnp.int32, (BLOCK, BLOCK), 0) < lax.broadcasted_iota(jnp.int32, (BLOCK, BLOCK), 1)
    rank = jnp.dot(kept.astype(BF), before.astype(jnp.float32).astype(BF), preferred_element_type=jnp.float32)
    slot = lax.broadcasted_iota(jnp.int32, (NB, BLOCK), 0) * SLOTS + rank.astype(jnp.int32)
    index[0:NB, :] = jnp.where(kept > 0.5, slot, ZERO)
    index[NB : NB + 8, :] = jnp.full((8, BLOCK), ZERO, jnp.int32)
    copy = pltpu.make_async_copy(index, table, sem)
    copy.start()
    copy.wait()
    for copy in from_cols + from_rows:
        copy.wait()

    def column(j, carry):
        def right(t, n):
            return rows[pl.ds(j * SLOTS + t, n)].reshape(n * BLOCK, BLOCK)

        result = product(table, [outer[j, s] for s in range(KS)], [inner[j, t] for t in range(KP)], cols, right)
        square[pl.ds(j * KS, KS)] = result.astype(BF).reshape(KS, SL, BLOCK)
        return carry

    lax.fori_loop(0, 4, column, 0)


def step_kernel(place, inner, table, *refs):
    row_parts, col_parts = refs[:NS], refs[NS : NS + NC]
    stepped, rows, cols, results, col_sems, row_sems, out_sems = refs[NS + NC :]
    from_cols = fetch_cols(place, col_parts, whole(COLS), cols, col_sems)
    from_rows = [
        fetch_rows(place, row_parts, column, rows, row_sems.at[j]) for j, column in enumerate(split(SQUARES, KS))
    ]
    for copy in from_cols + sum(from_rows, []):
        copy.start()
    for copy in from_cols:
        copy.wait()
    out = []
    for j in range(4):
        for copy in from_rows[j]:
            copy.wait()

        def right(t, n):
            return rows[j * KS + t : j * KS + t + n].reshape(n * BLOCK, BLOCK)

        outer = [inner[4 + j, s] for s in range(KT)]
        second = product(table, outer, [inner[j, t] for t in range(KS)], cols, right)
        if j >= 2:
            out[j - 2].wait()
        result = results.at[j % 2]
        result[...] = jnp.zeros_like(result)
        for s, i in enumerate(outer):
            own = cols[table[place[1] * 4 + j, i]].astype(jnp.float32)
            result[i] = (1.5 * own - 0.5 * second[s * SL : (s + 1) * SL]).astype(BF)
        out.append(
            pltpu.make_async_copy(
                result.at[pl.ds(0, NB)], stepped.at[:, :, pl.ds(j * BLOCK, BLOCK)], out_sems.at[j]
            )
        )
        out[j].start()
    out[2].wait()
    out[3].wait()


def square_rows_kernel(place, lists, *refs):
    row_parts = refs[:NS]
    out, rows, sems = refs[NS:]
    copies = fetch_rows(place, row_parts, whole(SQUARES), rows, sems)
    for copy in copies:
        copy.start()
    out[...] = jnp.zeros_like(out)
    for copy in copies:
        copy.wait()
    for j in range(4):

        def one(s, carry):
            i = lists[j, s]

            @pl.when(i // 8 == place[0])
            def _():
                out[i % 8, :, :, j * BLOCK : (j + 1) * BLOCK] = rows[j * KS + s]

            return carry

        lax.fori_loop(0, KS, one, 0)


SMEM = pl.BlockSpec(memory_space=pltpu.SMEM)
VMEM = pl.BlockSpec(memory_space=pltpu.VMEM)
ANY = pl.BlockSpec(memory_space=pl.ANY)


def column_block(rows, columns):
    return pl.BlockSpec((1, rows, columns), lambda j: (j, 0, 0))


def call(kernel, outs, in_specs, out_specs, scratch, flops, moved, grid=()):
    return pl.pallas_call(
        kernel,
        grid=grid,
        out_shape=outs,
        in_specs=in_specs,
        out_specs=out_specs,
        scratch_shapes=scratch,
        compiler_params=pltpu.CompilerParams(vmem_limit_bytes=VMEM_LIMIT),
        cost_estimate=pl.CostEstimate(flops=flops, bytes_accessed=moved, transcendentals=0),
    )


def apart(slots):
    half = slots // 2
    whole = [(0, 0), (0, 1), (1, 0), (3, 0), (1, 1), (3, 1)]
    layout = [[(0, back, line, 0, slots)] for back, line in whole]
    return layout + [[(0, 2, line, at, half)] for line in range(2) for at in (0, half)]


def merged(slots):
    half = slots // 2
    layout = [[(0, back, line, 0, slots)] for back, line in [(0, 0), (0, 1), (1, 0), (3, 0)]]
    layout += [[(0, 1, 1, 0, slots), (slots, 2, 0, 0, half)], [(0, 3, 1, 0, slots), (slots, 2, 0, half, half)]]
    return layout + [[(0, 2, 1, 0, half)], [(0, 2, 1, half, half)]]


def merged_cores(slots):
    mine = merged(slots)
    swapped = [mine[0], join(mine[1:4]), mine[4], mine[5], join(mine[6:8])]
    return mine + [[(start, back, line + 2, at, size) for start, back, line, at, size in part] for part in swapped]


def join(parts):
    out, begin = [], 0
    for part in parts:
        out += [(begin + start, back, line, at, size) for start, back, line, at, size in part]
        begin += sum(piece[4] for piece in part)
    return out


def ring_apart(packed, shift):
    half = packed.shape[0] // 2
    other = shift(packed, 0, 1)
    left, right = shift(packed, 1, 0), shift(packed, -1, 0)
    other_left, other_right = shift(other, 1, 0), shift(other, -1, 0)
    far = [shift(left[:half], 1, 0), shift(right[half:], -1, 0)]
    far += [shift(other_left[:half], 1, 0), shift(other_right[half:], -1, 0)]
    return [packed, other, left, right, other_left, other_right] + far


def ring_merged(packed, shift):
    slots = packed.shape[0]
    half = slots // 2
    other = shift(packed, 0, 1)
    left, right = shift(packed, 1, 0), shift(packed, -1, 0)
    from_left = shift(jnp.concatenate([other, left[:half]]), 1, 0)
    from_right = shift(jnp.concatenate([other, right[half:]]), -1, 0)
    far = [shift(from_left[:half], 1, 0), shift(from_right[half:slots], -1, 0)]
    return [packed, other, left, right, from_left, from_right] + far


def gather_rows(packed):
    return ring_apart(packed, row_shift)


def gather_cols(packed):
    mine = ring_merged(packed, lambda value, dz, dy: col_shift(value, dz, dy, 0))
    own = [mine[0], jnp.concatenate(mine[1:4]), mine[4], mine[5], jnp.concatenate(mine[6:8])]
    return mine + [col_shift(part, 0, 0, 1) for part in own]


ROWS = merged(PACK)
COLS = merged_cores(PACK)
SQUARES = apart(4 * KS)
NR, NC, NS = len(ROWS), len(COLS), len(SQUARES)


def pieces(layout):
    return sum(len(part) for part in layout)


def on_device(density, pattern, square_filter, step_filter):
    place = jnp.stack([lax.axis_index("row"), lax.axis_index("col")]).astype(jnp.int32)
    sent = call(
        slice_kernel,
        jax.ShapeDtypeStruct((TR, 33, SL, BLOCK), BF),
        [ANY] * 4,
        VMEM,
        [pltpu.VMEM((SL, BLOCK), jnp.float32), pltpu.VMEM((3, 4, 8), jnp.int32), pltpu.SemaphoreType.DMA((4 * TR + 3,))],
        0,
        2 << 20,
    )(density.reshape(8, TR, SL, 4 * BLOCK), pattern.T, square_filter.T, step_filter.T)
    sliced = lax.all_to_all(sent, "row", 0, 0, tiled=True)

    packed, pattern_lists, flags = call(
        pack_kernel,
        (
            jax.ShapeDtypeStruct((PACK, SL, BLOCK), BF),
            jax.ShapeDtypeStruct((4, 32), jnp.int32),
            jax.ShapeDtypeStruct((SL, BLOCK), jnp.int32),
        ),
        [VMEM],
        (VMEM, SMEM, VMEM),
        [pltpu.SMEM((SL, BLOCK), jnp.int32), pltpu.SemaphoreType.DMA],
        0,
        2 << 20,
    )(sliced)
    row_parts = ring_merged(packed, row_shift)
    col_parts = gather_cols(packed)
    lists = call(
        lists_kernel, jax.ShapeDtypeStruct((8, 32), jnp.int32), [SMEM] + [ANY] * NC, SMEM, [], 1048576, 12582912
    )(flags, *col_parts)
    square_packed, table = call(
        square_kernel,
        (
            jax.ShapeDtypeStruct((4 * KS, SL, BLOCK), BF),
            jax.ShapeDtypeStruct((NB + 8, BLOCK), jnp.int32),
        ),
        [SMEM] * 3 + [ANY] * (NR + NC),
        (VMEM, SMEM),
        [
            pltpu.VMEM((PACK, TR, SL, BLOCK), BF),
            pltpu.VMEM((TC * PACK, SL, BLOCK), BF),
            pltpu.VMEM((NB, BLOCK), jnp.float32),
            pltpu.VMEM((TC, SL, BLOCK), BF),
            pltpu.VMEM((NB + 8, BLOCK), jnp.int32),
            pltpu.SemaphoreType.DMA((pieces(COLS),)),
            pltpu.SemaphoreType.DMA((pieces(ROWS),)),
            pltpu.SemaphoreType.DMA((TC,)),
            pltpu.SemaphoreType.DMA,
        ],
        2 * 4 * KS * SL * KP * BLOCK * BLOCK,
        9 << 20,
    )(place, pattern_lists, lists, *row_parts, *col_parts)

    square_parts = gather_rows(square_packed)
    stepped = call(
        step_kernel,
        jax.ShapeDtypeStruct((NB, SL, 4 * BLOCK), BF),
        [SMEM] * 3 + [ANY] * (NS + NC),
        ANY,
        [
            pltpu.VMEM((4 * KS, TR, SL, BLOCK), BF),
            pltpu.VMEM((TC * PACK, SL, BLOCK), BF),
            pltpu.VMEM((2, NB + 8, SL, BLOCK), BF),
            pltpu.SemaphoreType.DMA((pieces(COLS),)),
            pltpu.SemaphoreType.DMA((4, TR)),
            pltpu.SemaphoreType.DMA((4,)),
        ],
        2 * 4 * KT * SL * KS * BLOCK * BLOCK,
        9 << 20,
    )(place, lists, table, *square_parts, *col_parts)
    back = lax.all_to_all(stepped, "row", 0, 0, tiled=True)
    square = call(
        square_rows_kernel,
        jax.ShapeDtypeStruct((8, TR, SL, 4 * BLOCK), BF),
        [SMEM, SMEM] + [ANY] * NS,
        VMEM,
        [pltpu.VMEM((4 * KS, TR, SL, BLOCK), BF), pltpu.SemaphoreType.DMA((pieces(SQUARES),))],
        0,
        4 << 20,
    )(place, lists, *square_parts)
    square = square.reshape(8 * BLOCK, 4 * BLOCK)
    stepped = back.reshape(TR, 8, SL, 4 * BLOCK).transpose(1, 0, 2, 3).reshape(8 * BLOCK, 4 * BLOCK)
    return square, stepped


def solution(mesh):
    placed = (P("row", "col"),) * 4
    return jax.shard_map(
        on_device,
        mesh=mesh,
        in_specs=placed,
        out_specs=(P("row", "col"), P("row", "col")),
        check_vma=False,
    )
```

```python
import functools

import jax
import jax.numpy as jnp
from jax import lax
from jax.experimental import pallas as pl
from jax.experimental.pallas import tpu as pltpu
from jax.sharding import PartitionSpec as P

BLOCK = 128
NB = 64
TR = 8
TC = 16
SL = 16
KP, KS, KT = 17, 25, 21
SLOTS = KP + 1
PACK = 4 * SLOTS
ZERO = PACK - 1
NONE = NB
VMEM_LIMIT = 60 * 1024 * 1024
BF = jnp.bfloat16


def row_index(x, y):
    return (x % 4) * 2 + (y % 2)


def col_index(z, y, core):
    return (z % 4) * 4 + (y % 2) * 2 + (core % 2)


def row_shift(value, dx, dy):
    pairs = [(row_index(x, y), row_index(x + dx, y + dy)) for x in range(4) for y in range(2)]
    return lax.ppermute(value, "row", pairs)


def col_shift(value, dz, dy, dc):
    pairs = [
        (col_index(z, y, c), col_index(z + dz, y + dy, c + dc))
        for z in range(4)
        for y in range(2)
        for c in range(2)
    ]
    return lax.ppermute(value, "col", pairs)


def slice_kernel(density, pattern, square_filter, step_filter, sent, small, masks, sems):
    copies = [
        pltpu.make_async_copy(density.at[:, d, :, pl.ds(n * BLOCK, BLOCK)], sent.at[d, pl.ds(8 * n, 8)], sems.at[4 * d + n])
        for d in range(TR)
        for n in range(4)
    ]
    filters = [
        pltpu.make_async_copy(mask, masks.at[n], sems.at[4 * TR + n])
        for n, mask in enumerate((pattern, square_filter, step_filter))
    ]
    for copy in filters + copies:
        copy.start()
    small[...] = jnp.zeros_like(small)
    for n, copy in enumerate(filters):
        copy.wait()
        small[4 * n : 4 * n + 4, 0:8] = masks[n].astype(jnp.float32)
    head = small[...].astype(BF)
    for d in range(TR):
        sent[d, 32] = head
    for copy in copies:
        copy.wait()


def pack_kernel(sliced, packed, flags, flags_s, sem):
    marks = jnp.zeros((SL, BLOCK), jnp.float32)
    for s in range(TR):
        mark = sliced[s, 32].astype(jnp.float32)
        marks = marks + (pltpu.roll(mark, 8 * s, 1) if s else mark)
    flags[...] = marks.astype(jnp.int32)
    copy = pltpu.make_async_copy(flags, flags_s, sem)
    copy.start()
    packed[...] = jnp.zeros_like(packed)
    copy.wait()

    def kept(b, counts):
        for q in range(8):
            i = 8 * b + q
            out = []
            for n in range(4):
                packed[n * SLOTS + counts[n]] = sliced[b, 8 * n + q]
                out.append(counts[n] + flags_s[n, i])
            counts = tuple(out)
        return counts

    lax.fori_loop(0, TR, kept, (jnp.int32(0),) * 4)
    packed[KP] = marks.astype(BF)
    packed[ZERO] = jnp.zeros((SL, BLOCK), BF)


def split(layout, slots):
    columns = [[] for _ in range(4)]
    for n, part in enumerate(layout):
        for start, back, line, at, size in part:
            for q in range(0, size, slots):
                columns[(at + q) // slots].append((n, start + q, back, line, at + q, slots))
    return columns


def whole(layout):
    return [(n, *piece) for n, part in enumerate(layout) for piece in part]


def fetch(parts, chosen, target, sems):
    copies = []
    for q, (n, start, back, line, at, size) in enumerate(chosen):
        copies.append(pltpu.make_async_copy(parts[n].at[pl.ds(start, size)], target(back, line, at, size), sems.at[q]))
    return copies


def fetch_rows(place, parts, chosen, rows, sems):
    x, y = place[0] // 2, place[0] % 2

    def target(back, line, at, size):
        return rows.at[pl.ds(at, size), lax.rem(x - back + 4, 4) * 2 + (y + line) % 2]

    return fetch(parts, chosen, target, sems)


def fetch_cols(place, parts, chosen, cols, sems):
    z, y, core = place[1] // 4, (place[1] // 2) % 2, place[1] % 2

    def target(back, line, at, size):
        line, other = line % 2, line // 2
        c = lax.rem(z - back + 4, 4) * 4 + ((y + line) % 2) * 2 + (core + other) % 2
        return cols.at[pl.ds(c * PACK + at, size)]

    return fetch(parts, chosen, target, sems)


def product(slot, n_outer, n_inner, cols, right):
    total = None
    for t in range(0, n_inner, 2):
        pair = range(t, min(t + 2, n_inner))
        left = jnp.concatenate(
            [jnp.concatenate([cols[slot(q, s)] for q in pair], axis=1) for s in range(n_outer)], axis=0
        )
        part = jnp.dot(left, right(t, len(pair)), preferred_element_type=jnp.float32)
        total = part if total is None else total + part
    return total


def exact_dot(left, right, contract=(1, 0)):
    dims = (((contract[0],), (contract[1],)), ((), ()))
    return lax.dot_general(left.astype(BF), right.astype(BF), dims, preferred_element_type=jnp.float32)


def picks(flags, ranks, first):
    at = lax.broadcasted_iota(jnp.int32, (32, BLOCK), 0).astype(jnp.float32)
    parts = []
    for n in range(first, first + 4):
        hit = (at == ranks[n : n + 1]) & (flags[n : n + 1] > 0.5)
        parts.append(jnp.where(hit, 1.0, 0.0))
    return jnp.concatenate(parts, axis=0)


def slots_of(inner, outer, high, low):
    parts = [exact_dot(exact_dot(inner, half), outer, (1, 1)) for half in (high, low)]
    found = 32.0 * parts[0] + parts[1]
    return jnp.where(found > 0.5, found - 1.0, float(ZERO)).astype(jnp.int32)


def fetch_heads(place, parts, heads, sems):
    z, y, core = place[1] // 4, (place[1] // 2) % 2, place[1] % 2
    copies = []
    for n, start, back, line, at, size in whole(COLS):
        if at <= KP < at + size:
            c = lax.rem(z - back + 4, 4) * 4 + ((y + line % 2) % 2) * 2 + (core + line // 2) % 2
            copies.append(pltpu.make_async_copy(parts[n].at[start + KP - at], heads.at[c], sems.at[len(copies)]))
    return copies


def plan_kernel(place, flags, *refs):
    square_slots, step_slots, lists, marks, heads, head_sems = refs[NC:]
    from_heads = fetch_heads(place, refs[:NC], heads, head_sems)
    for copy in from_heads:
        copy.start()
    line = lax.broadcasted_iota(jnp.int32, (BLOCK, BLOCK), 0)
    lane = lax.broadcasted_iota(jnp.int32, (BLOCK, BLOCK), 1)
    before = jnp.where(line < lane, 1.0, 0.0)
    mine = flags[...].astype(jnp.float32)
    ranks = exact_dot(mine, before)
    of_pattern, of_square, of_step = (picks(mine, ranks, n) for n in (0, 4, 8))
    own = (line % 32 == 31) & (lane == place[1] * 4 + line // 32)
    of_step_inner = jnp.where(own, 1.0, of_square)
    names = (line + 1).astype(jnp.float32)
    found = exact_dot(of_square, jnp.where(lane < NB, names, 0.0)) + exact_dot(of_step, jnp.where(lane < NB, 0.0, names))
    lists[...] = jnp.where(found > 0.5, found - 1.0, float(NONE)).astype(jnp.int32)
    marks[...] = jnp.zeros_like(marks)
    for copy in from_heads:
        copy.wait()
    for c in range(TC):
        marks[4 * c : 4 * c + 4, :] = heads[c].astype(jnp.float32)[0:4]
    kept = marks[...]
    rank = exact_dot(kept, before).astype(jnp.int32)
    slot = jnp.where(kept > 0.5, line * SLOTS + rank + 1, 0)
    high = (slot // 32).astype(jnp.float32)
    low = (slot % 32).astype(jnp.float32)
    square_slots[...] = slots_of(of_pattern, of_square, high, low)
    step_slots[...] = slots_of(of_step_inner, of_step, high, low)


def square_kernel(place, square_slots, *refs):
    row_parts, col_parts = refs[:NR], refs[NR : NR + NC]
    square, rows, cols, slots, col_sems, row_sems, sem = refs[NR + NC :]
    from_slots = pltpu.make_async_copy(square_slots, slots, sem)
    from_cols = fetch_cols(place, col_parts, whole(COLS), cols, col_sems)
    from_rows = fetch_rows(place, row_parts, whole(ROWS), rows, row_sems)
    for copy in [from_slots] + from_cols + from_rows:
        copy.start()
    for copy in [from_slots] + from_cols + from_rows:
        copy.wait()

    def column(j, carry):
        def right(t, n):
            return rows[pl.ds(j * SLOTS + t, n)].reshape(n * BLOCK, BLOCK)

        result = product(lambda t, s: slots[j * 32 + t, j * 32 + s], KS, KP, cols, right)
        square[pl.ds(j * KS, KS)] = result.astype(BF).reshape(KS, SL, BLOCK)
        return carry

    lax.fori_loop(0, 4, column, 0)


def step_kernel(place, all_lists, step_slots, *refs):
    row_parts, col_parts = refs[:NS], refs[NS : NS + NC]
    stepped, rows, cols, results, slots, lists, col_sems, row_sems, out_sems, sems = refs[NS + NC :]
    from_cols = fetch_cols(place, col_parts, whole(COLS), cols, col_sems)
    from_rows = [
        fetch_rows(place, row_parts, column, rows, row_sems.at[j]) for j, column in enumerate(split(SQUARES, KS))
    ]
    tables = [
        pltpu.make_async_copy(step_slots, slots, sems.at[0]),
        pltpu.make_async_copy(all_lists, lists, sems.at[1]),
    ]
    for copy in tables + from_cols + sum(from_rows, []):
        copy.start()
    for copy in tables + from_cols:
        copy.wait()
    out = []
    for j in range(4):
        for copy in from_rows[j]:
            copy.wait()

        def right(t, n):
            return rows[j * KS + t : j * KS + t + n].reshape(n * BLOCK, BLOCK)

        second = product(lambda t, s: slots[j * 32 + t, j * 32 + s], KT, KS, cols, right)
        if j >= 2:
            out[j - 2].wait()
        result = results.at[j % 2]
        result[...] = jnp.zeros_like(result)
        for s in range(KT):
            own = cols[slots[j * 32 + 31, j * 32 + s]].astype(jnp.float32)
            result[lists[32 * j + s, NB]] = (1.5 * own - 0.5 * second[s * SL : (s + 1) * SL]).astype(BF)
        out.append(
            pltpu.make_async_copy(
                result.at[pl.ds(0, NB)], stepped.at[:, :, pl.ds(j * BLOCK, BLOCK)], out_sems.at[j]
            )
        )
        out[j].start()
    out[2].wait()
    out[3].wait()


def square_rows_kernel(place, lists, *refs):
    row_parts = refs[:NS]
    out, rows, sems = refs[NS:]
    copies = fetch_rows(place, row_parts, whole(SQUARES), rows, sems)
    for copy in copies:
        copy.start()
    out[...] = jnp.zeros_like(out)
    for copy in copies:
        copy.wait()
    for j in range(4):

        def one(s, carry):
            i = lists[32 * j + s, 0]

            @pl.when(i // 8 == place[0])
            def _():
                out[i % 8, :, :, j * BLOCK : (j + 1) * BLOCK] = rows[j * KS + s]

            return carry

        lax.fori_loop(0, KS, one, 0)


SMEM = pl.BlockSpec(memory_space=pltpu.SMEM)
VMEM = pl.BlockSpec(memory_space=pltpu.VMEM)
ANY = pl.BlockSpec(memory_space=pl.ANY)


def column_block(rows, columns):
    return pl.BlockSpec((1, rows, columns), lambda j: (j, 0, 0))


def call(kernel, outs, in_specs, out_specs, scratch, flops, moved, grid=()):
    return pl.pallas_call(
        kernel,
        grid=grid,
        out_shape=outs,
        in_specs=in_specs,
        out_specs=out_specs,
        scratch_shapes=scratch,
        compiler_params=pltpu.CompilerParams(vmem_limit_bytes=VMEM_LIMIT),
        cost_estimate=pl.CostEstimate(flops=flops, bytes_accessed=moved, transcendentals=0),
    )


def apart(slots):
    half = slots // 2
    whole = [(0, 0), (0, 1), (1, 0), (3, 0), (1, 1), (3, 1)]
    layout = [[(0, back, line, 0, slots)] for back, line in whole]
    return layout + [[(0, 2, line, at, half)] for line in range(2) for at in (0, half)]


def merged(slots):
    half = slots // 2
    layout = [[(0, back, line, 0, slots)] for back, line in [(0, 0), (0, 1), (1, 0), (3, 0)]]
    layout += [[(0, 1, 1, 0, slots), (slots, 2, 0, 0, half)], [(0, 3, 1, 0, slots), (slots, 2, 0, half, half)]]
    return layout + [[(0, 2, 1, 0, half)], [(0, 2, 1, half, half)]]


def merged_cores(slots):
    mine = merged(slots)
    swapped = [mine[0], join(mine[1:4]), mine[4], mine[5], join(mine[6:8])]
    return mine + [[(start, back, line + 2, at, size) for start, back, line, at, size in part] for part in swapped]


def join(parts):
    out, begin = [], 0
    for part in parts:
        out += [(begin + start, back, line, at, size) for start, back, line, at, size in part]
        begin += sum(piece[4] for piece in part)
    return out


def ring_apart(packed, shift):
    half = packed.shape[0] // 2
    other = shift(packed, 0, 1)
    left, right = shift(packed, 1, 0), shift(packed, -1, 0)
    other_left, other_right = shift(other, 1, 0), shift(other, -1, 0)
    far = [shift(left[:half], 1, 0), shift(right[half:], -1, 0)]
    far += [shift(other_left[:half], 1, 0), shift(other_right[half:], -1, 0)]
    return [packed, other, left, right, other_left, other_right] + far


def ring_merged(packed, shift):
    slots = packed.shape[0]
    half = slots // 2
    other = shift(packed, 0, 1)
    left, right = shift(packed, 1, 0), shift(packed, -1, 0)
    from_left = shift(jnp.concatenate([other, left[:half]]), 1, 0)
    from_right = shift(jnp.concatenate([other, right[half:]]), -1, 0)
    far = [shift(from_left[:half], 1, 0), shift(from_right[half:slots], -1, 0)]
    return [packed, other, left, right, from_left, from_right] + far


def gather_rows(packed):
    return ring_apart(packed, row_shift)


def gather_cols(packed):
    mine = ring_merged(packed, lambda value, dz, dy: col_shift(value, dz, dy, 0))
    own = [mine[0], jnp.concatenate(mine[1:4]), mine[4], mine[5], jnp.concatenate(mine[6:8])]
    return mine + [col_shift(part, 0, 0, 1) for part in own]


ROWS = merged(PACK)
COLS = merged_cores(PACK)
SQUARES = apart(4 * KS)
NR, NC, NS = len(ROWS), len(COLS), len(SQUARES)


def pieces(layout):
    return sum(len(part) for part in layout)


def on_device(density, pattern, square_filter, step_filter):
    place = jnp.stack([lax.axis_index("row"), lax.axis_index("col")]).astype(jnp.int32)
    sent = call(
        slice_kernel,
        jax.ShapeDtypeStruct((TR, 33, SL, BLOCK), BF),
        [ANY] * 4,
        VMEM,
        [pltpu.VMEM((SL, BLOCK), jnp.float32), pltpu.VMEM((3, 4, 8), jnp.int32), pltpu.SemaphoreType.DMA((4 * TR + 3,))],
        0,
        2 << 20,
    )(density.reshape(8, TR, SL, 4 * BLOCK), pattern.T, square_filter.T, step_filter.T)
    sliced = lax.all_to_all(sent, "row", 0, 0, tiled=True)

    packed, flags = call(
        pack_kernel,
        (
            jax.ShapeDtypeStruct((PACK, SL, BLOCK), BF),
            jax.ShapeDtypeStruct((SL, BLOCK), jnp.int32),
        ),
        [VMEM],
        (VMEM, VMEM),
        [pltpu.SMEM((SL, BLOCK), jnp.int32), pltpu.SemaphoreType.DMA],
        0,
        2 << 20,
    )(sliced)
    row_parts = ring_merged(packed, row_shift)
    col_parts = gather_cols(packed)
    table = jax.ShapeDtypeStruct((BLOCK, BLOCK), jnp.int32)
    square_slots, step_slots, lists = call(
        plan_kernel,
        (table, table, table),
        [SMEM, VMEM] + [ANY] * NC,
        (VMEM, VMEM, VMEM),
        [
            pltpu.VMEM((BLOCK, BLOCK), jnp.float32),
            pltpu.VMEM((TC, SL, BLOCK), BF),
            pltpu.SemaphoreType.DMA((TC,)),
        ],
        1048576,
        12582912,
    )(place, flags, *col_parts)
    square_packed = call(
        square_kernel,
        jax.ShapeDtypeStruct((4 * KS, SL, BLOCK), BF),
        [SMEM] + [ANY] * (1 + NR + NC),
        VMEM,
        [
            pltpu.VMEM((PACK, TR, SL, BLOCK), BF),
            pltpu.VMEM((TC * PACK, SL, BLOCK), BF),
            pltpu.SMEM((BLOCK, BLOCK), jnp.int32),
            pltpu.SemaphoreType.DMA((pieces(COLS),)),
            pltpu.SemaphoreType.DMA((pieces(ROWS),)),
            pltpu.SemaphoreType.DMA,
        ],
        2 * 4 * KS * SL * KP * BLOCK * BLOCK,
        9 << 20,
    )(place, square_slots, *row_parts, *col_parts)

    square_parts = gather_rows(square_packed)
    stepped = call(
        step_kernel,
        jax.ShapeDtypeStruct((NB, SL, 4 * BLOCK), BF),
        [SMEM] + [ANY] * (2 + NS + NC),
        ANY,
        [
            pltpu.VMEM((4 * KS, TR, SL, BLOCK), BF),
            pltpu.VMEM((TC * PACK, SL, BLOCK), BF),
            pltpu.VMEM((2, NB + 8, SL, BLOCK), BF),
            pltpu.SMEM((BLOCK, BLOCK), jnp.int32),
            pltpu.SMEM((BLOCK, BLOCK), jnp.int32),
            pltpu.SemaphoreType.DMA((pieces(COLS),)),
            pltpu.SemaphoreType.DMA((4, TR)),
            pltpu.SemaphoreType.DMA((4,)),
            pltpu.SemaphoreType.DMA((2,)),
        ],
        2 * 4 * KT * SL * KS * BLOCK * BLOCK,
        9 << 20,
    )(place, lists, step_slots, *square_parts, *col_parts)
    back = lax.all_to_all(stepped, "row", 0, 0, tiled=True)
    square = call(
        square_rows_kernel,
        jax.ShapeDtypeStruct((8, TR, SL, 4 * BLOCK), BF),
        [SMEM, SMEM] + [ANY] * NS,
        VMEM,
        [pltpu.VMEM((4 * KS, TR, SL, BLOCK), BF), pltpu.SemaphoreType.DMA((pieces(SQUARES),))],
        0,
        4 << 20,
    )(place, lists, *square_parts)
    square = square.reshape(8 * BLOCK, 4 * BLOCK)
    stepped = back.reshape(TR, 8, SL, 4 * BLOCK).transpose(1, 0, 2, 3).reshape(8 * BLOCK, 4 * BLOCK)
    return square, stepped


def solution(mesh):
    placed = (P("row", "col"),) * 4
    return jax.shard_map(
        on_device,
        mesh=mesh,
        in_specs=placed,
        out_specs=(P("row", "col"), P("row", "col")),
        check_vma=False,
    )
```

```python
import functools

import jax
import jax.numpy as jnp
from jax import lax
from jax.experimental import pallas as pl
from jax.experimental.pallas import tpu as pltpu
from jax.sharding import PartitionSpec as P

BLOCK = 128
NB = 64
TR = 8
TC = 16
SL = 16
KP, KS, KT = 17, 25, 21
SLOTS = KP + 1
PACK = 4 * SLOTS
ZERO = PACK - 1
NONE = NB
VMEM_LIMIT = 60 * 1024 * 1024
BF = jnp.bfloat16


def row_index(x, y):
    return (x % 4) * 2 + (y % 2)


def col_index(z, y, core):
    return (z % 4) * 4 + (y % 2) * 2 + (core % 2)


def row_shift(value, dx, dy):
    pairs = [(row_index(x, y), row_index(x + dx, y + dy)) for x in range(4) for y in range(2)]
    return lax.ppermute(value, "row", pairs)


def col_shift(value, dz, dy, dc):
    pairs = [
        (col_index(z, y, c), col_index(z + dz, y + dy, c + dc))
        for z in range(4)
        for y in range(2)
        for c in range(2)
    ]
    return lax.ppermute(value, "col", pairs)


def slice_kernel(density, pattern, square_filter, step_filter, sent, small, masks, sems):
    copies = [
        pltpu.make_async_copy(density.at[:, d, :, pl.ds(n * BLOCK, BLOCK)], sent.at[d, pl.ds(8 * n, 8)], sems.at[4 * d + n])
        for d in range(TR)
        for n in range(4)
    ]
    filters = [
        pltpu.make_async_copy(mask, masks.at[n], sems.at[4 * TR + n])
        for n, mask in enumerate((pattern, square_filter, step_filter))
    ]
    for copy in filters + copies:
        copy.start()
    small[...] = jnp.zeros_like(small)
    for n, copy in enumerate(filters):
        copy.wait()
        small[4 * n : 4 * n + 4, 0:8] = masks[n].astype(jnp.float32)
    head = small[...].astype(BF)
    for d in range(TR):
        sent[d, 32] = head
    for copy in copies:
        copy.wait()


def pack_kernel(sliced, packed, flags, flags_s, sem):
    marks = jnp.zeros((SL, BLOCK), jnp.float32)
    for s in range(TR):
        mark = sliced[s, 32].astype(jnp.float32)
        marks = marks + (pltpu.roll(mark, 8 * s, 1) if s else mark)
    flags[...] = marks.astype(jnp.int32)
    copy = pltpu.make_async_copy(flags, flags_s, sem)
    copy.start()
    packed[...] = jnp.zeros_like(packed)
    copy.wait()

    def kept(b, counts):
        for q in range(8):
            i = 8 * b + q
            out = []
            for n in range(4):
                packed[n * SLOTS + counts[n]] = sliced[b, 8 * n + q]
                out.append(counts[n] + flags_s[n, i])
            counts = tuple(out)
        return counts

    lax.fori_loop(0, TR, kept, (jnp.int32(0),) * 4)
    packed[KP] = marks.astype(BF)
    packed[ZERO] = jnp.zeros((SL, BLOCK), BF)


def split(layout, slots):
    columns = [[] for _ in range(4)]
    for n, part in enumerate(layout):
        for start, back, line, at, size in part:
            for q in range(0, size, slots):
                columns[(at + q) // slots].append((n, start + q, back, line, at + q, slots))
    return columns


def whole(layout):
    return [(n, *piece) for n, part in enumerate(layout) for piece in part]


def fetch(parts, chosen, target, sems):
    copies = []
    for q, (n, start, back, line, at, size) in enumerate(chosen):
        copies.append(pltpu.make_async_copy(parts[n].at[pl.ds(start, size)], target(back, line, at, size), sems.at[q]))
    return copies


def fetch_rows(place, parts, chosen, rows, sems):
    x, y = place[0] // 2, place[0] % 2

    def target(back, line, at, size):
        return rows.at[pl.ds(at, size), lax.rem(x - back + 4, 4) * 2 + (y + line) % 2]

    return fetch(parts, chosen, target, sems)


def fetch_cols(place, parts, chosen, cols, sems):
    z, y, core = place[1] // 4, (place[1] // 2) % 2, place[1] % 2

    def target(back, line, at, size):
        line, other = line % 2, line // 2
        c = lax.rem(z - back + 4, 4) * 4 + ((y + line) % 2) * 2 + (core + other) % 2
        return cols.at[pl.ds(c * PACK + at, size)]

    return fetch(parts, chosen, target, sems)


def product(slot, n_outer, n_inner, cols, right):
    total = None
    for t in range(0, n_inner, 2):
        pair = range(t, min(t + 2, n_inner))
        left = jnp.concatenate(
            [jnp.concatenate([cols[slot(q, s)] for q in pair], axis=1) for s in range(n_outer)], axis=0
        )
        part = jnp.dot(left, right(t, len(pair)), preferred_element_type=jnp.float32)
        total = part if total is None else total + part
    return total


def exact_dot(left, right, contract=(1, 0)):
    dims = (((contract[0],), (contract[1],)), ((), ()))
    return lax.dot_general(left.astype(BF), right.astype(BF), dims, preferred_element_type=jnp.float32)


def picks(flags, ranks, first):
    at = lax.broadcasted_iota(jnp.int32, (32, BLOCK), 0).astype(jnp.float32)
    parts = []
    for n in range(first, first + 4):
        hit = (at == ranks[n : n + 1]) & (flags[n : n + 1] > 0.5)
        parts.append(jnp.where(hit, 1.0, 0.0))
    return jnp.concatenate(parts, axis=0)


def slots_of(inner, outer, high, low):
    parts = [exact_dot(exact_dot(inner, half), outer, (1, 1)) for half in (high, low)]
    found = 32.0 * parts[0] + parts[1]
    return jnp.where(found > 0.5, found - 1.0, float(ZERO)).astype(jnp.int32)


def fetch_heads(place, parts, heads, sems):
    z, y, core = place[1] // 4, (place[1] // 2) % 2, place[1] % 2
    copies = []
    for n, start, back, line, at, size in whole(COLS):
        if at <= KP < at + size:
            c = lax.rem(z - back + 4, 4) * 4 + ((y + line % 2) % 2) * 2 + (core + line // 2) % 2
            copies.append(pltpu.make_async_copy(parts[n].at[start + KP - at], heads.at[c], sems.at[len(copies)]))
    return copies


def plan_kernel(place, flags, *refs):
    square_slots, step_slots, lists, marks, heads, head_sems = refs[NC:]
    from_heads = fetch_heads(place, refs[:NC], heads, head_sems)
    for copy in from_heads:
        copy.start()
    line = lax.broadcasted_iota(jnp.int32, (BLOCK, BLOCK), 0)
    lane = lax.broadcasted_iota(jnp.int32, (BLOCK, BLOCK), 1)
    before = jnp.where(line < lane, 1.0, 0.0)
    mine = flags[...].astype(jnp.float32)
    ranks = exact_dot(mine, before)
    of_pattern, of_square, of_step = (picks(mine, ranks, n) for n in (0, 4, 8))
    own = (line % 32 == 31) & (lane == place[1] * 4 + line // 32)
    of_step_inner = jnp.where(own, 1.0, of_square)
    names = (line + 1).astype(jnp.float32)
    found = exact_dot(of_square, jnp.where(lane < NB, names, 0.0)) + exact_dot(of_step, jnp.where(lane < NB, 0.0, names))
    lists[...] = jnp.where(found > 0.5, found - 1.0, float(NONE)).astype(jnp.int32)
    marks[...] = jnp.zeros_like(marks)
    for copy in from_heads:
        copy.wait()
    for c in range(TC):
        marks[4 * c : 4 * c + 4, :] = heads[c].astype(jnp.float32)[0:4]
    kept = marks[...]
    rank = exact_dot(kept, before).astype(jnp.int32)
    slot = jnp.where(kept > 0.5, line * SLOTS + rank + 1, 0)
    high = (slot // 32).astype(jnp.float32)
    low = (slot % 32).astype(jnp.float32)
    square_slots[...] = slots_of(of_pattern, of_square, high, low)
    step_slots[...] = slots_of(of_step_inner, of_step, high, low)


def square_kernel(place, square_slots, *refs):
    row_parts, col_parts = refs[:NR], refs[NR : NR + NC]
    square, rows, cols, slots, col_sems, row_sems, sem = refs[NR + NC :]
    from_slots = pltpu.make_async_copy(square_slots, slots, sem)
    from_cols = fetch_cols(place, col_parts, whole(COLS), cols, col_sems)
    from_rows = fetch_rows(place, row_parts, whole(ROWS), rows, row_sems)
    for copy in [from_slots] + from_cols + from_rows:
        copy.start()
    for copy in [from_slots] + from_cols + from_rows:
        copy.wait()

    def column(j, carry):
        def right(t, n):
            return rows[pl.ds(j * SLOTS + t, n)].reshape(n * BLOCK, BLOCK)

        result = product(lambda t, s: slots[j * 32 + t, j * 32 + s], KS, KP, cols, right)
        square[pl.ds(j * KS, KS)] = result.astype(BF).reshape(KS, SL, BLOCK)
        return carry

    for j in range(4):
        column(j, 0)


def step_kernel(place, all_lists, step_slots, *refs):
    row_parts, col_parts = refs[:NS], refs[NS : NS + NC]
    stepped, rows, cols, results, slots, lists, col_sems, row_sems, out_sems, sems = refs[NS + NC :]
    from_cols = fetch_cols(place, col_parts, whole(COLS), cols, col_sems)
    from_rows = [
        fetch_rows(place, row_parts, column, rows, row_sems.at[j]) for j, column in enumerate(split(SQUARES, KS))
    ]
    tables = [
        pltpu.make_async_copy(step_slots, slots, sems.at[0]),
        pltpu.make_async_copy(all_lists, lists, sems.at[1]),
    ]
    for copy in tables + from_cols + sum(from_rows, []):
        copy.start()
    for n in range(4):
        results[n] = jnp.zeros_like(results[n])
    for copy in tables + from_cols + sum(from_rows, []):
        copy.wait()
    out = []
    for j in range(4):

        def right(t, n):
            return rows[j * KS + t : j * KS + t + n].reshape(n * BLOCK, BLOCK)

        second = product(lambda t, s: slots[j * 32 + t, j * 32 + s], KT, KS, cols, right)
        result = results.at[j]
        for s in range(KT):
            own = cols[slots[j * 32 + 31, j * 32 + s]].astype(jnp.float32)
            result[lists[32 * j + s, NB]] = (1.5 * own - 0.5 * second[s * SL : (s + 1) * SL]).astype(BF)
        out.append(
            pltpu.make_async_copy(
                result.at[pl.ds(0, NB)], stepped.at[:, :, pl.ds(j * BLOCK, BLOCK)], out_sems.at[j]
            )
        )
        out[j].start()
    for copy in out:
        copy.wait()


def square_rows_kernel(place, lists, *refs):
    row_parts = refs[:NS]
    out, rows, sems = refs[NS:]
    copies = fetch_rows(place, row_parts, whole(SQUARES), rows, sems)
    for copy in copies:
        copy.start()
    out[...] = jnp.zeros_like(out)
    for copy in copies:
        copy.wait()
    for j in range(4):

        def one(s, carry):
            i = lists[32 * j + s, 0]

            @pl.when(i // 8 == place[0])
            def _():
                out[i % 8, :, :, j * BLOCK : (j + 1) * BLOCK] = rows[j * KS + s]

            return carry

        lax.fori_loop(0, KS, one, 0)


SMEM = pl.BlockSpec(memory_space=pltpu.SMEM)
VMEM = pl.BlockSpec(memory_space=pltpu.VMEM)
ANY = pl.BlockSpec(memory_space=pl.ANY)


def column_block(rows, columns):
    return pl.BlockSpec((1, rows, columns), lambda j: (j, 0, 0))


def call(kernel, outs, in_specs, out_specs, scratch, flops, moved, grid=()):
    return pl.pallas_call(
        kernel,
        grid=grid,
        out_shape=outs,
        in_specs=in_specs,
        out_specs=out_specs,
        scratch_shapes=scratch,
        compiler_params=pltpu.CompilerParams(vmem_limit_bytes=VMEM_LIMIT),
        cost_estimate=pl.CostEstimate(flops=flops, bytes_accessed=moved, transcendentals=0),
    )


def apart(slots):
    half = slots // 2
    whole = [(0, 0), (0, 1), (1, 0), (3, 0), (1, 1), (3, 1)]
    layout = [[(0, back, line, 0, slots)] for back, line in whole]
    return layout + [[(0, 2, line, at, half)] for line in range(2) for at in (0, half)]


def crossed(slots):
    half = slots // 2
    layout = [[(0, back, line, 0, slots)] for back, line in [(0, 0), (0, 1), (1, 0), (3, 0)]]
    layout += [[(0, 1, 1, 0, half)], [(0, 2, 0, 0, half)], [(0, 3, 1, half, half)], [(0, 2, 0, half, half)]]
    layout += [[(0, 3, 1, 0, half), (half, 1, 1, half, half)]]
    return layout + [[(0, 2, 1, 0, half)], [(0, 2, 1, half, half)]]


def merged(slots):
    half = slots // 2
    layout = [[(0, back, line, 0, slots)] for back, line in [(0, 0), (0, 1), (1, 0), (3, 0)]]
    layout += [[(0, 1, 1, 0, slots), (slots, 2, 0, 0, half)], [(0, 3, 1, 0, slots), (slots, 2, 0, half, half)]]
    return layout + [[(0, 2, 1, 0, half)], [(0, 2, 1, half, half)]]


def merged_cores(slots):
    mine = merged(slots)
    swapped = [mine[0], join(mine[1:4]), mine[4], mine[5], join(mine[6:8])]
    return mine + [[(start, back, line + 2, at, size) for start, back, line, at, size in part] for part in swapped]


def join(parts):
    out, begin = [], 0
    for part in parts:
        out += [(begin + start, back, line, at, size) for start, back, line, at, size in part]
        begin += sum(piece[4] for piece in part)
    return out


def ring_apart(packed, shift):
    half = packed.shape[0] // 2
    other = shift(packed, 0, 1)
    left, right = shift(packed, 1, 0), shift(packed, -1, 0)
    other_left, other_right = shift(other, 1, 0), shift(other, -1, 0)
    far = [shift(left[:half], 1, 0), shift(right[half:], -1, 0)]
    far += [shift(other_left[:half], 1, 0), shift(other_right[half:], -1, 0)]
    return [packed, other, left, right, other_left, other_right] + far


def ring_merged(packed, shift):
    slots = packed.shape[0]
    half = slots // 2
    other = shift(packed, 0, 1)
    left, right = shift(packed, 1, 0), shift(packed, -1, 0)
    from_left = shift(jnp.concatenate([other, left[:half]]), 1, 0)
    from_right = shift(jnp.concatenate([other, right[half:]]), -1, 0)
    far = [shift(from_left[:half], 1, 0), shift(from_right[half:slots], -1, 0)]
    return [packed, other, left, right, from_left, from_right] + far


def gather_rows(packed):
    half = packed.shape[0] // 2
    other = row_shift(packed, 0, 1)
    left, right = row_shift(packed, 1, 0), row_shift(packed, -1, 0)
    other_left, other_right = row_shift(other[:half], 1, 0), row_shift(other[half:], -1, 0)
    near = [other_left, row_shift(left[:half], 1, 0), other_right, row_shift(right[half:], -1, 0)]
    far = [row_shift(other_left, 1, 0), row_shift(other_right, -1, 0)]
    cross = row_shift(jnp.concatenate([right[:half], left[half:]]), 0, 1)
    return [packed, other, left, right, *near, cross, *far]


def gather_cols(packed):
    mine = ring_merged(packed, lambda value, dz, dy: col_shift(value, dz, dy, 0))
    own = [mine[0], jnp.concatenate(mine[1:4]), mine[4], mine[5], jnp.concatenate(mine[6:8])]
    return mine + [col_shift(part, 0, 0, 1) for part in own]


ROWS = merged(PACK)
COLS = merged_cores(PACK)
SQUARES = crossed(4 * KS)
NR, NC, NS = len(ROWS), len(COLS), len(SQUARES)


def pieces(layout):
    return sum(len(part) for part in layout)


def on_device(density, pattern, square_filter, step_filter):
    place = jnp.stack([lax.axis_index("row"), lax.axis_index("col")]).astype(jnp.int32)
    sent = call(
        slice_kernel,
        jax.ShapeDtypeStruct((TR, 33, SL, BLOCK), BF),
        [ANY] * 4,
        VMEM,
        [pltpu.VMEM((SL, BLOCK), jnp.float32), pltpu.VMEM((3, 4, 8), jnp.int32), pltpu.SemaphoreType.DMA((4 * TR + 3,))],
        0,
        2 << 20,
    )(density.reshape(8, TR, SL, 4 * BLOCK), pattern.T, square_filter.T, step_filter.T)
    sliced = lax.all_to_all(sent, "row", 0, 0, tiled=True)

    packed, flags = call(
        pack_kernel,
        (
            jax.ShapeDtypeStruct((PACK, SL, BLOCK), BF),
            jax.ShapeDtypeStruct((SL, BLOCK), jnp.int32),
        ),
        [VMEM],
        (VMEM, VMEM),
        [pltpu.SMEM((SL, BLOCK), jnp.int32), pltpu.SemaphoreType.DMA],
        0,
        2 << 20,
    )(sliced)
    row_parts = ring_merged(packed, row_shift)
    col_parts = gather_cols(packed)
    table = jax.ShapeDtypeStruct((BLOCK, BLOCK), jnp.int32)
    square_slots, step_slots, lists = call(
        plan_kernel,
        (table, table, table),
        [SMEM, VMEM] + [ANY] * NC,
        (VMEM, VMEM, VMEM),
        [
            pltpu.VMEM((BLOCK, BLOCK), jnp.float32),
            pltpu.VMEM((TC, SL, BLOCK), BF),
            pltpu.SemaphoreType.DMA((TC,)),
        ],
        1048576,
        12582912,
    )(place, flags, *col_parts)
    square_packed = call(
        square_kernel,
        jax.ShapeDtypeStruct((4 * KS, SL, BLOCK), BF),
        [SMEM] + [ANY] * (1 + NR + NC),
        VMEM,
        [
            pltpu.VMEM((PACK, TR, SL, BLOCK), BF),
            pltpu.VMEM((TC * PACK, SL, BLOCK), BF),
            pltpu.SMEM((BLOCK, BLOCK), jnp.int32),
            pltpu.SemaphoreType.DMA((pieces(COLS),)),
            pltpu.SemaphoreType.DMA((pieces(ROWS),)),
            pltpu.SemaphoreType.DMA,
        ],
        2 * 4 * KS * SL * KP * BLOCK * BLOCK,
        9 << 20,
    )(place, square_slots, *row_parts, *col_parts)

    square_parts = gather_rows(square_packed)
    stepped = call(
        step_kernel,
        jax.ShapeDtypeStruct((NB, SL, 4 * BLOCK), BF),
        [SMEM] + [ANY] * (2 + NS + NC),
        ANY,
        [
            pltpu.VMEM((4 * KS, TR, SL, BLOCK), BF),
            pltpu.VMEM((TC * PACK, SL, BLOCK), BF),
            pltpu.VMEM((4, NB + 8, SL, BLOCK), BF),
            pltpu.SMEM((BLOCK, BLOCK), jnp.int32),
            pltpu.SMEM((BLOCK, BLOCK), jnp.int32),
            pltpu.SemaphoreType.DMA((pieces(COLS),)),
            pltpu.SemaphoreType.DMA((4, 16)),
            pltpu.SemaphoreType.DMA((4,)),
            pltpu.SemaphoreType.DMA((2,)),
        ],
        2 * 4 * KT * SL * KS * BLOCK * BLOCK,
        9 << 20,
    )(place, lists, step_slots, *square_parts, *col_parts)
    back = lax.all_to_all(stepped, "row", 0, 0, tiled=True)
    square = call(
        square_rows_kernel,
        jax.ShapeDtypeStruct((8, TR, SL, 4 * BLOCK), BF),
        [SMEM, SMEM] + [ANY] * NS,
        VMEM,
        [pltpu.VMEM((4 * KS, TR, SL, BLOCK), BF), pltpu.SemaphoreType.DMA((pieces(SQUARES),))],
        0,
        4 << 20,
    )(place, lists, *square_parts)
    square = square.reshape(8 * BLOCK, 4 * BLOCK)
    stepped = back.reshape(TR, 8, SL, 4 * BLOCK).transpose(1, 0, 2, 3).reshape(8 * BLOCK, 4 * BLOCK)
    return square, stepped


def solution(mesh):
    placed = (P("row", "col"),) * 4
    return jax.shard_map(
        on_device,
        mesh=mesh,
        in_specs=placed,
        out_specs=(P("row", "col"), P("row", "col")),
        check_vma=False,
    )
```

```python
import functools

import jax
import jax.numpy as jnp
from jax import lax
from jax.experimental import pallas as pl
from jax.experimental.pallas import tpu as pltpu
from jax.sharding import PartitionSpec as P

BLOCK = 128
NB = 64
TR = 8
TC = 16
SL = 16
KP, KS, KT = 17, 25, 21
SLOTS = KP + 1
PACK = 4 * SLOTS
ZERO = PACK - 1
NONE = NB
VMEM_LIMIT = 60 * 1024 * 1024
BF = jnp.bfloat16


def row_index(x, y):
    return (x % 4) * 2 + (y % 2)


def col_index(z, y, core):
    return (z % 4) * 4 + (y % 2) * 2 + (core % 2)


def row_shift(value, dx, dy):
    pairs = [(row_index(x, y), row_index(x + dx, y + dy)) for x in range(4) for y in range(2)]
    return lax.ppermute(value, "row", pairs)


def col_shift(value, dz, dy, dc):
    pairs = [
        (col_index(z, y, c), col_index(z + dz, y + dy, c + dc))
        for z in range(4)
        for y in range(2)
        for c in range(2)
    ]
    return lax.ppermute(value, "col", pairs)


def slice_kernel(density, pattern, square_filter, step_filter, sent, small, masks, sems):
    copies = [
        pltpu.make_async_copy(density.at[:, d, :, pl.ds(n * BLOCK, BLOCK)], sent.at[d, pl.ds(8 * n, 8)], sems.at[4 * d + n])
        for d in range(TR)
        for n in range(4)
    ]
    filters = [
        pltpu.make_async_copy(mask, masks.at[n], sems.at[4 * TR + n])
        for n, mask in enumerate((pattern, square_filter, step_filter))
    ]
    for copy in filters + copies:
        copy.start()
    small[...] = jnp.zeros_like(small)
    for n, copy in enumerate(filters):
        copy.wait()
        small[4 * n : 4 * n + 4, 0:8] = masks[n].astype(jnp.float32)
    head = small[...].astype(BF)
    for d in range(TR):
        sent[d, 32] = head
    for copy in copies:
        copy.wait()


def pack_kernel(sliced, packed, flags, flags_s, sem):
    marks = jnp.zeros((SL, BLOCK), jnp.float32)
    for s in range(TR):
        mark = sliced[s, 32].astype(jnp.float32)
        marks = marks + (pltpu.roll(mark, 8 * s, 1) if s else mark)
    flags[...] = marks.astype(jnp.int32)
    copy = pltpu.make_async_copy(flags, flags_s, sem)
    copy.start()
    packed[...] = jnp.zeros_like(packed)
    copy.wait()

    counts = [jnp.int32(0)] * 4
    for i in range(NB):
        for n in range(4):
            packed[n * SLOTS + counts[n]] = sliced[i // 8, 8 * n + i % 8]
            counts[n] = counts[n] + flags_s[n, i]
    packed[KP] = marks.astype(BF)
    packed[ZERO] = jnp.zeros((SL, BLOCK), BF)


def split(layout, slots):
    columns = [[] for _ in range(4)]
    for n, part in enumerate(layout):
        for start, back, line, at, size in part:
            for q in range(0, size, slots):
                columns[(at + q) // slots].append((n, start + q, back, line, at + q, slots))
    return columns


def whole(layout):
    return [(n, *piece) for n, part in enumerate(layout) for piece in part]


def fetch(parts, chosen, target, sems):
    copies = []
    for q, (n, start, back, line, at, size) in enumerate(chosen):
        copies.append(pltpu.make_async_copy(parts[n].at[pl.ds(start, size)], target(back, line, at, size), sems.at[q]))
    return copies


def fetch_rows(place, parts, chosen, rows, sems):
    x, y = place[0] // 2, place[0] % 2

    def target(back, line, at, size):
        return rows.at[pl.ds(at, size), lax.rem(x - back + 4, 4) * 2 + (y + line) % 2]

    return fetch(parts, chosen, target, sems)


def fetch_cols(place, parts, chosen, cols, sems):
    z, y, core = place[1] // 4, (place[1] // 2) % 2, place[1] % 2

    def target(back, line, at, size):
        line, other = line % 2, line // 2
        c = lax.rem(z - back + 4, 4) * 4 + ((y + line) % 2) * 2 + (core + other) % 2
        return cols.at[pl.ds(c * PACK + at, size)]

    return fetch(parts, chosen, target, sems)


def product(slot, n_outer, n_inner, cols, right):
    total = None
    for t in range(0, n_inner, 2):
        pair = range(t, min(t + 2, n_inner))
        left = jnp.concatenate(
            [jnp.concatenate([cols[slot(q, s)] for q in pair], axis=1) for s in range(n_outer)], axis=0
        )
        part = jnp.dot(left, right(t, len(pair)), preferred_element_type=jnp.float32)
        total = part if total is None else total + part
    return total


def exact_dot(left, right, contract=(1, 0)):
    dims = (((contract[0],), (contract[1],)), ((), ()))
    return lax.dot_general(left.astype(BF), right.astype(BF), dims, preferred_element_type=jnp.float32)


def picks(flags, ranks, first):
    at = lax.broadcasted_iota(jnp.int32, (32, BLOCK), 0).astype(jnp.float32)
    parts = []
    for n in range(first, first + 4):
        hit = (at == ranks[n : n + 1]) & (flags[n : n + 1] > 0.5)
        parts.append(jnp.where(hit, 1.0, 0.0))
    return jnp.concatenate(parts, axis=0)


def slots_of(inner, outer, high, low):
    parts = [exact_dot(exact_dot(inner, half), outer, (1, 1)) for half in (high, low)]
    found = 32.0 * parts[0] + parts[1]
    return jnp.where(found > 0.5, found - 1.0, float(ZERO)).astype(jnp.int32)


def fetch_heads(place, parts, heads, sems):
    z, y, core = place[1] // 4, (place[1] // 2) % 2, place[1] % 2
    copies = []
    for n, start, back, line, at, size in whole(COLS):
        if at <= KP < at + size:
            c = lax.rem(z - back + 4, 4) * 4 + ((y + line % 2) % 2) * 2 + (core + line // 2) % 2
            copies.append(pltpu.make_async_copy(parts[n].at[start + KP - at], heads.at[c], sems.at[len(copies)]))
    return copies


def plan_kernel(place, flags, *refs):
    square_slots, step_slots, lists, marks, heads, head_sems = refs[NC:]
    from_heads = fetch_heads(place, refs[:NC], heads, head_sems)
    for copy in from_heads:
        copy.start()
    line = lax.broadcasted_iota(jnp.int32, (BLOCK, BLOCK), 0)
    lane = lax.broadcasted_iota(jnp.int32, (BLOCK, BLOCK), 1)
    before = jnp.where(line < lane, 1.0, 0.0)
    mine = flags[...].astype(jnp.float32)
    ranks = exact_dot(mine, before)
    of_pattern, of_square, of_step = (picks(mine, ranks, n) for n in (0, 4, 8))
    own = (line % 32 == 31) & (lane == place[1] * 4 + line // 32)
    of_step_inner = jnp.where(own, 1.0, of_square)
    names = (line + 1).astype(jnp.float32)
    found = exact_dot(of_square, jnp.where(lane < NB, names, 0.0)) + exact_dot(of_step, jnp.where(lane < NB, 0.0, names))
    lists[...] = jnp.where(found > 0.5, found - 1.0, float(NONE)).astype(jnp.int32)
    marks[...] = jnp.zeros_like(marks)
    for copy in from_heads:
        copy.wait()
    for c in range(TC):
        marks[4 * c : 4 * c + 4, :] = heads[c].astype(jnp.float32)[0:4]
    kept = marks[...]
    rank = exact_dot(kept, before).astype(jnp.int32)
    slot = jnp.where(kept > 0.5, line * SLOTS + rank + 1, 0)
    high = (slot // 32).astype(jnp.float32)
    low = (slot % 32).astype(jnp.float32)
    square_slots[...] = slots_of(of_pattern, of_square, high, low)
    step_slots[...] = slots_of(of_step_inner, of_step, high, low)


def square_kernel(place, square_slots, *refs):
    row_parts, col_parts = refs[:NR], refs[NR : NR + NC]
    square, rows, cols, slots, col_sems, row_sems, sem = refs[NR + NC :]
    from_slots = pltpu.make_async_copy(square_slots, slots, sem)
    from_cols = fetch_cols(place, col_parts, whole(COLS), cols, col_sems)
    from_rows = fetch_rows(place, row_parts, whole(ROWS), rows, row_sems)
    for copy in [from_slots] + from_cols + from_rows:
        copy.start()
    for copy in [from_slots] + from_cols + from_rows:
        copy.wait()

    def column(j, carry):
        def right(t, n):
            return rows[pl.ds(j * SLOTS + t, n)].reshape(n * BLOCK, BLOCK)

        result = product(lambda t, s: slots[j * 32 + t, j * 32 + s], KS, KP, cols, right)
        square[pl.ds(j * KS, KS)] = result.astype(BF).reshape(KS, SL, BLOCK)
        return carry

    for j in range(4):
        column(j, 0)


def step_kernel(place, all_lists, step_slots, *refs):
    row_parts, col_parts = refs[:NS], refs[NS : NS + NC]
    stepped, rows, cols, results, slots, lists, col_sems, row_sems, out_sems, sems = refs[NS + NC :]
    from_cols = fetch_cols(place, col_parts, whole(COLS), cols, col_sems)
    from_rows = [
        fetch_rows(place, row_parts, column, rows, row_sems.at[j]) for j, column in enumerate(split(SQUARES, KS))
    ]
    tables = [
        pltpu.make_async_copy(step_slots, slots, sems.at[0]),
        pltpu.make_async_copy(all_lists, lists, sems.at[1]),
    ]
    for copy in tables + from_cols + sum(from_rows, []):
        copy.start()
    for n in range(4):
        results[n] = jnp.zeros_like(results[n])
    for copy in tables + from_cols + sum(from_rows, []):
        copy.wait()
    out = []
    for j in range(4):

        def right(t, n):
            return rows[j * KS + t : j * KS + t + n].reshape(n * BLOCK, BLOCK)

        second = product(lambda t, s: slots[j * 32 + t, j * 32 + s], KT, KS, cols, right)
        result = results.at[j]
        for s in range(KT):
            own = cols[slots[j * 32 + 31, j * 32 + s]].astype(jnp.float32)
            result[lists[32 * j + s, NB]] = (1.5 * own - 0.5 * second[s * SL : (s + 1) * SL]).astype(BF)
        out.append(
            pltpu.make_async_copy(
                result.at[pl.ds(0, NB)], stepped.at[:, :, pl.ds(j * BLOCK, BLOCK)], out_sems.at[j]
            )
        )
        out[j].start()
    for copy in out:
        copy.wait()


def square_rows_kernel(place, lists, *refs):
    row_parts = refs[:NS]
    out, rows, sems = refs[NS:]
    copies = fetch_rows(place, row_parts, whole(SQUARES), rows, sems)
    for copy in copies:
        copy.start()
    out[...] = jnp.zeros_like(out)
    for copy in copies:
        copy.wait()
    for j in range(4):

        def one(s, carry):
            i = lists[32 * j + s, 0]

            @pl.when(i // 8 == place[0])
            def _():
                out[i % 8, :, :, j * BLOCK : (j + 1) * BLOCK] = rows[j * KS + s]

            return carry

        lax.fori_loop(0, KS, one, 0)


SMEM = pl.BlockSpec(memory_space=pltpu.SMEM)
VMEM = pl.BlockSpec(memory_space=pltpu.VMEM)
ANY = pl.BlockSpec(memory_space=pl.ANY)


def column_block(rows, columns):
    return pl.BlockSpec((1, rows, columns), lambda j: (j, 0, 0))


def call(kernel, outs, in_specs, out_specs, scratch, flops, moved, grid=()):
    return pl.pallas_call(
        kernel,
        grid=grid,
        out_shape=outs,
        in_specs=in_specs,
        out_specs=out_specs,
        scratch_shapes=scratch,
        compiler_params=pltpu.CompilerParams(vmem_limit_bytes=VMEM_LIMIT),
        cost_estimate=pl.CostEstimate(flops=flops, bytes_accessed=moved, transcendentals=0),
    )


def apart(slots):
    half = slots // 2
    whole = [(0, 0), (0, 1), (1, 0), (3, 0), (1, 1), (3, 1)]
    layout = [[(0, back, line, 0, slots)] for back, line in whole]
    return layout + [[(0, 2, line, at, half)] for line in range(2) for at in (0, half)]


def crossed(slots):
    half = slots // 2
    layout = [[(0, back, line, 0, slots)] for back, line in [(0, 0), (0, 1), (1, 0), (3, 0)]]
    layout += [[(0, 1, 1, 0, half)], [(0, 2, 0, 0, half)], [(0, 3, 1, half, half)], [(0, 2, 0, half, half)]]
    layout += [[(0, 3, 1, 0, half), (half, 1, 1, half, half)]]
    return layout + [[(0, 2, 1, 0, half)], [(0, 2, 1, half, half)]]


def merged(slots):
    half = slots // 2
    layout = [[(0, back, line, 0, slots)] for back, line in [(0, 0), (0, 1), (1, 0), (3, 0)]]
    layout += [[(0, 1, 1, 0, slots), (slots, 2, 0, 0, half)], [(0, 3, 1, 0, slots), (slots, 2, 0, half, half)]]
    return layout + [[(0, 2, 1, 0, half)], [(0, 2, 1, half, half)]]


def merged_cores(slots):
    mine = merged(slots)
    swapped = [mine[0], join(mine[1:4]), mine[4], mine[5], join(mine[6:8])]
    return mine + [[(start, back, line + 2, at, size) for start, back, line, at, size in part] for part in swapped]


def join(parts):
    out, begin = [], 0
    for part in parts:
        out += [(begin + start, back, line, at, size) for start, back, line, at, size in part]
        begin += sum(piece[4] for piece in part)
    return out


def ring_apart(packed, shift):
    half = packed.shape[0] // 2
    other = shift(packed, 0, 1)
    left, right = shift(packed, 1, 0), shift(packed, -1, 0)
    other_left, other_right = shift(other, 1, 0), shift(other, -1, 0)
    far = [shift(left[:half], 1, 0), shift(right[half:], -1, 0)]
    far += [shift(other_left[:half], 1, 0), shift(other_right[half:], -1, 0)]
    return [packed, other, left, right, other_left, other_right] + far


def ring_merged(packed, shift):
    slots = packed.shape[0]
    half = slots // 2
    other = shift(packed, 0, 1)
    left, right = shift(packed, 1, 0), shift(packed, -1, 0)
    from_left = shift(jnp.concatenate([other, left[:half]]), 1, 0)
    from_right = shift(jnp.concatenate([other, right[half:]]), -1, 0)
    far = [shift(from_left[:half], 1, 0), shift(from_right[half:slots], -1, 0)]
    return [packed, other, left, right, from_left, from_right] + far


def gather_rows(packed):
    half = packed.shape[0] // 2
    other = row_shift(packed, 0, 1)
    left, right = row_shift(packed, 1, 0), row_shift(packed, -1, 0)
    other_left, other_right = row_shift(other[:half], 1, 0), row_shift(other[half:], -1, 0)
    near = [other_left, row_shift(left[:half], 1, 0), other_right, row_shift(right[half:], -1, 0)]
    far = [row_shift(other_left, 1, 0), row_shift(other_right, -1, 0)]
    cross = row_shift(jnp.concatenate([right[:half], left[half:]]), 0, 1)
    return [packed, other, left, right, *near, cross, *far]


def gather_cols(packed):
    mine = ring_merged(packed, lambda value, dz, dy: col_shift(value, dz, dy, 0))
    own = [mine[0], jnp.concatenate(mine[1:4]), mine[4], mine[5], jnp.concatenate(mine[6:8])]
    return mine + [col_shift(part, 0, 0, 1) for part in own]


ROWS = merged(PACK)
COLS = merged_cores(PACK)
SQUARES = crossed(4 * KS)
NR, NC, NS = len(ROWS), len(COLS), len(SQUARES)


def pieces(layout):
    return sum(len(part) for part in layout)


def on_device(density, pattern, square_filter, step_filter):
    place = jnp.stack([lax.axis_index("row"), lax.axis_index("col")]).astype(jnp.int32)
    sent = call(
        slice_kernel,
        jax.ShapeDtypeStruct((TR, 33, SL, BLOCK), BF),
        [ANY] * 4,
        VMEM,
        [pltpu.VMEM((SL, BLOCK), jnp.float32), pltpu.VMEM((3, 4, 8), jnp.int32), pltpu.SemaphoreType.DMA((4 * TR + 3,))],
        0,
        2 << 20,
    )(density.reshape(8, TR, SL, 4 * BLOCK), pattern.T, square_filter.T, step_filter.T)
    sliced = lax.all_to_all(sent, "row", 0, 0, tiled=True)

    packed, flags = call(
        pack_kernel,
        (
            jax.ShapeDtypeStruct((PACK, SL, BLOCK), BF),
            jax.ShapeDtypeStruct((SL, BLOCK), jnp.int32),
        ),
        [VMEM],
        (VMEM, VMEM),
        [pltpu.SMEM((SL, BLOCK), jnp.int32), pltpu.SemaphoreType.DMA],
        0,
        2 << 20,
    )(sliced)
    row_parts = ring_merged(packed, row_shift)
    col_parts = gather_cols(packed)
    table = jax.ShapeDtypeStruct((BLOCK, BLOCK), jnp.int32)
    square_slots, step_slots, lists = call(
        plan_kernel,
        (table, table, table),
        [SMEM, VMEM] + [ANY] * NC,
        (VMEM, VMEM, VMEM),
        [
            pltpu.VMEM((BLOCK, BLOCK), jnp.float32),
            pltpu.VMEM((TC, SL, BLOCK), BF),
            pltpu.SemaphoreType.DMA((TC,)),
        ],
        1048576,
        12582912,
    )(place, flags, *col_parts)
    square_packed = call(
        square_kernel,
        jax.ShapeDtypeStruct((4 * KS, SL, BLOCK), BF),
        [SMEM] + [ANY] * (1 + NR + NC),
        VMEM,
        [
            pltpu.VMEM((PACK, TR, SL, BLOCK), BF),
            pltpu.VMEM((TC * PACK, SL, BLOCK), BF),
            pltpu.SMEM((BLOCK, BLOCK), jnp.int32),
            pltpu.SemaphoreType.DMA((pieces(COLS),)),
            pltpu.SemaphoreType.DMA((pieces(ROWS),)),
            pltpu.SemaphoreType.DMA,
        ],
        2 * 4 * KS * SL * KP * BLOCK * BLOCK,
        9 << 20,
    )(place, square_slots, *row_parts, *col_parts)

    square_parts = gather_rows(square_packed)
    stepped = call(
        step_kernel,
        jax.ShapeDtypeStruct((NB, SL, 4 * BLOCK), BF),
        [SMEM] + [ANY] * (2 + NS + NC),
        ANY,
        [
            pltpu.VMEM((4 * KS, TR, SL, BLOCK), BF),
            pltpu.VMEM((TC * PACK, SL, BLOCK), BF),
            pltpu.VMEM((4, NB + 8, SL, BLOCK), BF),
            pltpu.SMEM((BLOCK, BLOCK), jnp.int32),
            pltpu.SMEM((BLOCK, BLOCK), jnp.int32),
            pltpu.SemaphoreType.DMA((pieces(COLS),)),
            pltpu.SemaphoreType.DMA((4, 16)),
            pltpu.SemaphoreType.DMA((4,)),
            pltpu.SemaphoreType.DMA((2,)),
        ],
        2 * 4 * KT * SL * KS * BLOCK * BLOCK,
        9 << 20,
    )(place, lists, step_slots, *square_parts, *col_parts)
    back = lax.all_to_all(stepped, "row", 0, 0, tiled=True)
    square = call(
        square_rows_kernel,
        jax.ShapeDtypeStruct((8, TR, SL, 4 * BLOCK), BF),
        [SMEM, SMEM] + [ANY] * NS,
        VMEM,
        [pltpu.VMEM((4 * KS, TR, SL, BLOCK), BF), pltpu.SemaphoreType.DMA((pieces(SQUARES),))],
        0,
        4 << 20,
    )(place, lists, *square_parts)
    square = square.reshape(8 * BLOCK, 4 * BLOCK)
    stepped = back.reshape(TR, 8, SL, 4 * BLOCK).transpose(1, 0, 2, 3).reshape(8 * BLOCK, 4 * BLOCK)
    return square, stepped


def solution(mesh):
    placed = (P("row", "col"),) * 4
    return jax.shard_map(
        on_device,
        mesh=mesh,
        in_specs=placed,
        out_specs=(P("row", "col"), P("row", "col")),
        check_vma=False,
    )
```
